256 devices in a mesh: run: 4 (over y), space: 64 (over z, x, core).
Axes of the slice: x: 4, y: 4, z: 8, core: 2. Of those that a mesh axis runs over, the one named last changes fastest.
Arguments:
- snapshots: bfloat16 [131072, 1024], P('space', 'run'), may hold values from -6 to 6
- run_counts: int32 [4], P('run'), may hold values from 128 to 256
- route_counts: int32 [64, 64], replicated, may hold values from 16 to 48, as said below
Outputs:
- modes: bfloat16 [131072, 256], P('space', 'run')
The draws below stay inside these ranges and needn't reach their ends.
Inputs may be any that keep to these rules, and one draw needn't show every extreme that they name: route_counts[s, d] depends only on (d - s) mod 64; each of its rows and columns sums to 2048.
All inputs are finite; a program needn't handle non-finite values.
Results may differ from the reference program's by a relative error of at most 0.0069.
The reference program's roundings to bfloat16 on the way count: a program that leaves them out, or rounds other values in their place, can miss the bound.
Values may be sent and summed in bfloat16 or wider, within the bound.
No kernel may reach another device: no remote copies, remote signals or barrier semaphores. Data moves between devices by JAX's collectives and lax.ppermute only.
A program may use at most 64 MiB of HBM per device.

```python
import math
import jax
import jax.numpy as jnp
from jax import lax

CELL_DEV = 2048
RANK = 256
LEVELS = 2
ITERS = 2
NS_STEPS = 8
RUNS = 4
SHARDS = 64
CELLS = 131072
SNAPS = 1024
N_RUN = 4


def draw_run_counts(key, part):
    key_a, key_b, key_c = jax.random.split(key, 3)
    values = jax.random.randint(key_a, (RUNS,), RANK // 2, RANK + 1)
    top_run = jax.random.randint(key_b, (), 0, RUNS)
    low_run = (top_run + 1 + jax.random.randint(key_c, (), 0, RUNS - 1)) % RUNS
    places = jnp.arange(RUNS)
    values = jnp.where(places == top_run, RANK, values)
    values = jnp.where(places == low_run, RANK // 2, values)
    return values.astype(jnp.int32)


def draw_route_counts(key, part):
    key_a, key_b = jax.random.split(jax.random.fold_in(key, 7), 2)
    base = CELL_DEV // SHARDS
    half = base // 2
    order = jax.random.permutation(key_a, SHARDS)
    amounts = jax.random.randint(key_b, (SHARDS // 2,), 0, half + 1)
    amounts = amounts.at[0].set(half)
    signed = jnp.concatenate([amounts, -amounts])
    delta = jnp.zeros((SHARDS,), jnp.int32).at[order].set(signed.astype(jnp.int32))
    weights = base + delta
    source = jnp.arange(SHARDS)[:, None]
    target = jnp.arange(SHARDS)[None, :]
    return weights[(target - source) % SHARDS].astype(jnp.int32)


def level_of(own_key, dims, cuts, least, high):
    def one(position, blocks):
        draws = jax.random.uniform(jax.random.fold_in(jax.random.fold_in(own_key, 6), position), (blocks,), jnp.float32, least / len(cuts), high / len(cuts))
        return jnp.repeat(jnp.exp(draws), dims[position] // blocks).reshape((-1,) + (1,) * (len(dims) - position - 1))

    gain = one(*cuts[0])
    for cut in cuts[1:]:
        gain = gain * one(*cut)
    return gain


def noise(key, dims, width, bound, cuts=(), kind=jnp.bfloat16):
    entries = jax.random.normal(key, dims, jnp.float32) * width
    if len(cuts) > 0:
        entries = level_of(key, dims, cuts, -0.22, 0.18) * entries
    return jnp.clip(entries, min=-bound, max=bound).astype(kind)


def setup_inputs(seed: int = 0) -> dict:
    key_list = jax.random.split(jax.random.key(seed), 4)
    return {
        "snapshots": noise(key_list[0], (CELLS, SNAPS), 1.0, 6.0, ((0, 64), (1, 4))),
        "run_counts": draw_run_counts(jax.random.fold_in(key_list[3], 71), 0),
        "route_counts": draw_route_counts(jax.random.fold_in(key_list[3], 71), 0),
    }


def arrange_rows(snapshots, route_counts):
    counts = route_counts.astype(jnp.int32)
    row_start = jnp.cumsum(counts, axis=1) - counts
    src_start = jnp.cumsum(counts, axis=0) - counts
    places = jnp.arange(CELL_DEV, dtype=jnp.int32)
    starts_t = src_start.T
    before = starts_t[:, None, :] <= places[None, :, None]
    source = (lax.optimization_barrier(jnp.sum(before.astype(jnp.int32), axis=2)) - 1).astype(jnp.int32)
    seg_begin = lax.optimization_barrier(jnp.max(jnp.where(before, starts_t[:, None, :], 0), axis=2))
    offsets = jnp.take_along_axis(row_start.T, source, axis=1)
    flat_index = source * CELL_DEV + offsets + places[None, :] - seg_begin
    return snapshots[flat_index.reshape(-1).astype(jnp.int32)]

def eigen_basis(gram):
    eye_block = jnp.eye(RANK, dtype=jnp.float32)
    rotation = jnp.concatenate([eye_block, eye_block], axis=0) / math.sqrt(2.0)
    for sweep_idx in range(ITERS):
        projected = jnp.dot(gram, rotation, precision=lax.Precision.HIGHEST)
        scaled = projected / jnp.sqrt(jnp.sum(projected * projected) + 1e-06)
        for inner_idx in range(NS_STEPS):
            moment = jnp.dot(scaled.T, scaled, precision=lax.Precision.HIGHEST)
            scaled = 1.5 * scaled - 0.5 * jnp.dot(scaled, moment, precision=lax.Precision.HIGHEST)
        rotation = scaled
    return rotation

def reference(snapshots, run_counts, route_counts):
    arranged = arrange_rows(snapshots, route_counts)
    columns = jnp.arange(SNAPS, dtype=jnp.int32)
    run_of = columns // RANK
    within = columns % RANK
    keep_cols = within < run_counts[run_of]
    masked = jnp.where(keep_cols[None, :], arranged, jnp.zeros((), arranged.dtype))
    factors = [masked[:, r * RANK:(r + 1) * RANK] for r in range(N_RUN)]
    for level in range(LEVELS):
        stride = 2 ** level
        merged = {}
        new_factors = []
        for r in range(N_RUN):
            first = min(r, r ^ stride)
            second = max(r, r ^ stride)
            if first not in merged:
                joined = jnp.concatenate([factors[first], factors[second]], axis=1)
                gram = jnp.dot(joined.T, joined, preferred_element_type=jnp.float32)
                rotation = eigen_basis(gram).astype(jnp.bfloat16)
                merged[first] = jnp.dot(joined, rotation, preferred_element_type=jnp.float32).astype(jnp.bfloat16)
            new_factors.append(merged[first])
        factors = new_factors
    quarter = RANK // N_RUN
    pieces = [factors[r][:, r * quarter:(r + 1) * quarter] for r in range(N_RUN)]
    return jnp.concatenate(pieces, axis=1)
```

```python
import functools
import math

import jax
import jax.numpy as jnp
from jax import lax
from jax.experimental import pallas as pl
from jax.experimental.pallas import tpu as pltpu
from jax.sharding import PartitionSpec as P

ITERS = 2
NS_STEPS = 8
BF = jnp.bfloat16
F32 = jnp.float32


def dot(a, b):
    return lax.dot_general(a, b, (((1,), (0,)), ((), ())), preferred_element_type=F32)


def dot_t(a, b):
    return lax.dot_general(a, b, (((0,), (0,)), ((), ())), preferred_element_type=F32)


def split(x):
    hi = x.astype(BF)
    return hi, (x - hi.astype(F32)).astype(BF)


def mul(a, b, op=dot):
    return op(a[0], b[0]) + (op(a[0], b[1]) + op(a[1], b[0]))


def half_mul(a, b, op=dot):
    return op(a[0], b) + op(a[1], b)


def half_mul_t(b, a):
    return dot_t(b, a[0]) + dot_t(b, a[1])


def solve(grams, eye, m_ref, t_ref):
    count = len(grams)
    root = 1.0 / math.sqrt(2.0)
    gs = [(split(a), split(b), split(c)) for a, b, c in grams]
    heads = [((a + b) * root, (b.T + c) * root) for a, b, c in grams]
    for sweep in range(ITERS):
        if sweep:
            nxt = []
            for (a, b, c), (xt, xb) in zip(gs, heads):
                st, sb = split(xt), split(xb)
                nxt.append((mul(a, st) + mul(b, sb), mul(b, st, dot_t) + mul(c, sb)))
            heads = nxt
        scaled = []
        for i, (pt, pb) in enumerate(heads):
            norm = jnp.sqrt(jnp.sum(pt * pt + pb * pb, keepdims=True) + 1e-06)
            st, sb = split(pt / norm), split(pb / norm)
            scaled.append((st, sb))
            moment = mul(st, st, dot_t) + mul(sb, sb, dot_t)
            m_ref[i] = moment
            t_ref[i] = eye

        def step(_, carry):
            for i in range(count):
                moment = m_ref[i]
                sm = split(moment)
                weight = 1.5 * eye - 0.5 * moment
                square = mul(sm, sm)
                t_ref[i] = mul(split(t_ref[i]), split(weight))
                m_ref[i] = mul(sm, split(2.25 * eye - 1.5 * moment + 0.25 * square))
            return carry

        lax.fori_loop(0, NS_STEPS - 1, step, 0)
        heads = []
        for i in range(count):
            weight = 1.5 * eye - 0.5 * m_ref[i]
            turn = split(mul(split(t_ref[i]), split(weight)))
            st, sb = scaled[i]
            heads.append((mul(st, turn), mul(sb, turn)))
    return heads


def eig_kernel(place_ref, *refs):
    parts, (own_ref, far_ref, last_ref, gram_ref, m_ref, t_ref, sems) = refs[:8], refs[8:]
    run, core = place_ref[0], place_ref[1]
    copies = []
    for j in range(4):
        for k in range(2):
            slot = core if k == 0 else 1 - core
            copies.append(pltpu.make_async_copy(parts[2 * j + k], gram_ref.at[j, slot], sems.at[2 * j + k]))
    for c in copies:
        c.start()
    for c in copies:
        c.wait()
    width = own_ref.shape[1]
    half = width // 2
    rows = lax.broadcasted_iota(jnp.int32, (width, width), 0)
    cols = lax.broadcasted_iota(jnp.int32, (width, width), 1)
    eye = (rows == cols).astype(F32)

    def diag(j):
        return gram_ref[j, 0, :, :width]

    def edge(j):
        return jnp.concatenate([gram_ref[j, 0, :, width:], gram_ref[j, 1, :, :half]], axis=1)

    def cross(j):
        return gram_ref[j, 1, :, half:]

    near = (diag(0), edge(0), diag(1))
    far = (diag(2), edge(2), diag(3))
    bases = [(t.astype(BF), b.astype(BF)) for t, b in solve([near, far], eye, m_ref, t_ref)]
    for ref, (t, b) in zip((own_ref, far_ref), bases):
        ref[:width] = t
        ref[width:] = b

    def turned(gram, basis):
        a, b, c = (split(g) for g in gram)
        t, s = basis
        up = half_mul(a, t) + half_mul(b, s)
        down = half_mul(b, t, dot_t) + half_mul(c, s)
        return half_mul_t(t, split(up)) + half_mul_t(s, split(down))

    def between(first, second, f0, f1, s0, s1):
        (ft, fb), (st, sb) = first, second
        to_s1, to_s0 = split(cross(f0)), split(cross(f1))
        from_s0, from_s1 = split(cross(s0)), split(cross(s1))
        up = half_mul(to_s1, sb) + half_mul(from_s1, st, dot_t)
        down = half_mul(to_s0, st) + half_mul(from_s0, sb, dot_t)
        return half_mul_t(ft, split(up)) + half_mul_t(fb, split(down))

    a1 = turned(near, bases[0])
    c1 = turned(far, bases[1])

    @pl.when(run < 2)
    def _():
        m_ref[0] = between(bases[0], bases[1], 0, 1, 2, 3)

    @pl.when(run >= 2)
    def _():
        m_ref[0] = between(bases[1], bases[0], 2, 3, 0, 1).T

    b1 = m_ref[0]
    [(t, b)] = solve([(a1, b1, c1)], eye, m_ref, t_ref)
    lanes = last_ref.shape[1]
    quarter = lanes // 2
    pick_row = lax.broadcasted_iota(jnp.int32, (width, lanes), 0)
    pick_col = lax.broadcasted_iota(jnp.int32, (width, lanes), 1)
    pick_col = jnp.where(pick_col >= quarter, pick_col - quarter, pick_col)
    pick = (pick_row == pick_col + run * quarter).astype(F32).astype(BF)
    last_ref[:width] = dot(t.astype(BF), pick).astype(BF)
    last_ref[width:] = dot(b.astype(BF), pick).astype(BF)


def eig(place, parts, width):
    return pl.pallas_call(
        eig_kernel,
        out_shape=[
            jax.ShapeDtypeStruct((2 * width, width), BF),
            jax.ShapeDtypeStruct((2 * width, width), BF),
            jax.ShapeDtypeStruct((2 * width, width // 2), BF),
        ],
        in_specs=[pl.BlockSpec(memory_space=pltpu.SMEM)] + [pl.BlockSpec(memory_space=pl.ANY)] * 8,
        scratch_shapes=[
            pltpu.VMEM((4, 2, width, 3 * width // 2), F32),
            pltpu.VMEM((2, width, width), F32),
            pltpu.VMEM((2, width, width), F32),
            pltpu.SemaphoreType.DMA((8,)),
        ],
        compiler_params=pltpu.CompilerParams(vmem_limit_bytes=40 * 2**20),
        cost_estimate=pl.CostEstimate(flops=20 * 10**9, bytes_accessed=4 * 2**20, transcendentals=0),
        name="eigensolves",
    )(place, *parts)


def pack_kernel(shards, slots, counts_ref, own_ref, p1_ref, p2a_ref, p2b_ref, p3_ref, near_ref, far_ref, last_ref,
                out_ref, rows_ref, slot_ref):
    width = own_ref.shape[1]
    cells = own_ref.shape[0]
    tile = 512
    for k in range(cells // tile):
        at = pl.ds(k * tile, tile)
        half = cells // 2
        p2 = p2a_ref[at] if k * tile < half else p2b_ref[pl.ds(k * tile - half, tile)]
        near = (dot(own_ref[at], near_ref[:width]) + dot(p1_ref[at], near_ref[width:])).astype(BF)
        far = (dot(p2, far_ref[:width]) + dot(p3_ref[at], far_ref[width:])).astype(BF)
        rows_ref[at] = dot(near, last_ref[:width]) + dot(far, last_ref[width:])
    pad = rows_ref.shape[0] - cells
    rows_ref[pl.ds(cells, pad)] = jnp.zeros((pad, rows_ref.shape[1]), F32)
    half_slot = slots // 2
    lane = lax.broadcasted_iota(jnp.int32, (half_slot, rows_ref.shape[1]), 1)

    def one(d, start):
        first = rows_ref[pl.ds(start, half_slot)]
        second = rows_ref[pl.ds(start + half_slot, half_slot)]
        slot_ref[pl.ds(pl.multiple_of(d * half_slot, 8), half_slot)] = jnp.where(
            lane < rows_ref.shape[1] // 2, first, second
        )
        return jnp.minimum(start + counts_ref[d], cells)

    lax.fori_loop(0, shards, one, jnp.int32(0))
    out_ref[...] = slot_ref[...].astype(BF)


def unpack_kernel(shards, slots, counts_ref, in_ref, out_ref, slot_ref, rows_ref):
    cells, quarter = out_ref.shape
    half_slot = slots // 2
    slot_ref[...] = in_ref[...].astype(F32)

    def one(s, start):
        pair = slot_ref[pl.ds(pl.multiple_of(s * half_slot, 8), half_slot)]
        rows_ref[pl.ds(start, half_slot)] = pair
        rows_ref[pl.ds(start + half_slot, half_slot)] = pltpu.roll(pair, quarter, 1)
        return jnp.minimum(start + counts_ref[s], cells)

    lax.fori_loop(0, shards, one, jnp.int32(0))
    out_ref[...] = rows_ref[pl.ds(0, cells), :quarter].astype(BF)


def body(snapshots, run_counts, route_counts):
    cells, width = snapshots.shape
    shards = lax.axis_size("space")
    runs = lax.axis_size("run")
    slots = 3 * cells // (2 * shards)
    run = lax.axis_index("run")
    spot = lax.axis_index("space")
    core = lax.rem(spot, 2)
    groups = [[2 * i + c for i in range(shards // 2)] for c in range(2)]

    def across(x, mask):
        return lax.ppermute(x, "run", [(r, r ^ mask) for r in range(runs)])

    def other_core(x):
        return lax.ppermute(x, "space", [(s, s ^ 1) for s in range(shards)])

    def opposite(p1, p3):
        half = p1.shape[0] // 2
        return across(p1[:half], 3), across(p3[half:], 1)

    keep = jnp.arange(width, dtype=jnp.int32) < run_counts[0]
    own = jnp.where(keep[None, :], snapshots, jnp.zeros((), BF))
    p1, p3 = across(own, 1), across(own, 3)
    p2a, p2b = opposite(p1, p3)

    left = jnp.where(run < 2, own, p1)
    local = jnp.concatenate([dot_t(own, own), dot_t(own, p1), dot_t(left, p3)], axis=1)
    cut = local.shape[1] // 2
    mine = jnp.where(core == 0, local[:, :cut], local[:, cut:])
    theirs = jnp.where(core == 0, local[:, cut:], local[:, :cut])
    mine = mine + other_core(theirs)
    pieces = mine.reshape(shards // 2, -1, cut)
    pieces = lax.all_to_all(pieces, "space", 0, 0, tiled=True, axis_index_groups=groups)
    total = jnp.sum(pieces, axis=0)
    pieces = lax.all_to_all(
        jnp.broadcast_to(total, pieces.shape), "space", 0, 0, tiled=True, axis_index_groups=groups
    )
    g0 = pieces.reshape(width, cut)
    g1, g3 = across(g0, 1), across(g0, 3)
    g2 = jnp.concatenate(opposite(g1, g3), axis=0)
    parts = []
    for g in (g0, g1, g2, g3):
        parts += [g, other_core(g)]
    place = jnp.stack([run, core]).astype(jnp.int32)
    near, far, last = eig(place, parts, width)

    send = lax.dynamic_index_in_dim(route_counts, spot, 0, keepdims=False)
    recv = lax.dynamic_index_in_dim(route_counts, spot, 1, keepdims=False)
    smem = pl.BlockSpec(memory_space=pltpu.SMEM)
    vmem = pl.BlockSpec(memory_space=pltpu.VMEM)
    lanes = width // 2
    flat = shards * slots // 2
    packed = pl.pallas_call(
        functools.partial(pack_kernel, shards, slots),
        out_shape=jax.ShapeDtypeStruct((flat, lanes), BF),
        in_specs=[smem] + [vmem] * 8,
        out_specs=vmem,
        scratch_shapes=[pltpu.VMEM((cells + 64, lanes), F32), pltpu.VMEM((flat, lanes), F32)],
        compiler_params=pltpu.CompilerParams(vmem_limit_bytes=40 * 2**20),
        name="rotate_and_pack",
    )(send, own, p1, p2a, p2b, p3, near, far, last)
    arrived = lax.all_to_all(packed.reshape(shards, slots // 2, lanes), "space", 0, 0, tiled=True)
    return pl.pallas_call(
        functools.partial(unpack_kernel, shards, slots),
        out_shape=jax.ShapeDtypeStruct((cells, width // runs), BF),
        in_specs=[smem, vmem],
        out_specs=vmem,
        scratch_shapes=[pltpu.VMEM((flat, lanes), F32), pltpu.VMEM((cells + 64, lanes), F32)],
        compiler_params=pltpu.CompilerParams(vmem_limit_bytes=40 * 2**20),
        name="unpack",
    )(recv, arrived.reshape(flat, lanes))


def solution(mesh):
    in_specs = (P("space", "run"), P("run"), P())
    out_specs = P("space", "run")
    return jax.shard_map(body, mesh=mesh, in_specs=in_specs, out_specs=out_specs, check_vma=False)
```

```python
import functools
import math

import jax
import jax.numpy as jnp
from jax import lax
from jax.experimental import pallas as pl
from jax.experimental.pallas import tpu as pltpu
from jax.sharding import PartitionSpec as P

ITERS = 2
NS_STEPS = 8
BF = jnp.bfloat16
F32 = jnp.float32


def dot(a, b):
    return lax.dot_general(a, b, (((1,), (0,)), ((), ())), preferred_element_type=F32)


def dot_t(a, b):
    return lax.dot_general(a, b, (((0,), (0,)), ((), ())), preferred_element_type=F32)


def split(x):
    hi = x.astype(BF)
    return hi, (x - hi.astype(F32)).astype(BF)


def mul(a, b, op=dot):
    return op(a[0], b[0]) + (op(a[0], b[1]) + op(a[1], b[0]))


def half_mul(a, b, op=dot):
    return op(a[0], b) + op(a[1], b)


def half_mul_t(b, a):
    return dot_t(b, a[0]) + dot_t(b, a[1])


def solve(grams, eye):
    root = 1.0 / math.sqrt(2.0)
    gs = [(split(a), split(b), split(c)) for a, b, c in grams]
    heads = [((a + b) * root, (b.T + c) * root) for a, b, c in grams]
    for sweep in range(ITERS):
        scaled = []
        for pt, pb in heads:
            norm = lax.rsqrt(jnp.sum(pt * pt + pb * pb, keepdims=True) + 1e-06)
            scaled.append((split(pt * norm), split(pb * norm)))
        moments = [mul(st, st, dot_t) + mul(sb, sb, dot_t) for st, sb in scaled]
        turns = None
        ahead, fill = [], []
        for (a, b, c), (st, sb) in zip(gs, scaled):
            cell = [None] * 4
            ahead.append(cell)
            for n, f in enumerate((lambda a=a, st=st: mul(a, st), lambda b=b, sb=sb: mul(b, sb),
                                   lambda b=b, st=st: mul(b, st, dot_t), lambda c=c, sb=sb: mul(c, sb))):
                fill.append((cell, n, f))
        if sweep + 1 == ITERS:
            fill = []
        for k in range(NS_STEPS):
            last = k == NS_STEPS - 1
            halves = [split(m) for m in moments]
            weights = [1.5 * eye - 0.5 * m for m in moments]
            if not last:
                squares = [mul(h, h) for h in halves]
            turns = weights if k == 0 else [mul(split(t), split(w)) for t, w in zip(turns, weights)]
            for cell, n, f in fill[:len(grams)]:
                cell[n] = f()
            fill = fill[len(grams):]
            if not last:
                moments = [mul(h, split(2.25 * eye - 1.5 * m + 0.25 * q)) for h, m, q in zip(halves, moments, squares)]
        turns = [split(t) for t in turns]
        if sweep + 1 < ITERS:
            scaled = [(split(c[0] + c[1]), split(c[2] + c[3])) for c in ahead]
        heads = [(mul(st, t), mul(sb, t)) for (st, sb), t in zip(scaled, turns)]
    return heads


def identity(width):
    rows = lax.broadcasted_iota(jnp.int32, (width, width), 0)
    return (rows == lax.broadcasted_iota(jnp.int32, (width, width), 1)).astype(F32)


def level0_kernel(place_ref, *refs):
    parts, (near_ref, far_ref, outer_ref, own_ref, p1_ref, p2_ref, p3_ref, sems) = refs[:8], refs[8:]
    core = place_ref[1]
    copies = []
    for j, ref in enumerate((own_ref, p1_ref, p2_ref, p3_ref)):
        for k, slot in enumerate((core, 1 - core)):
            copies.append(pltpu.make_async_copy(parts[2 * j + k], ref.at[slot], sems.at[2 * j + k]))
    for c in copies:
        c.start()
    for c in copies:
        c.wait()
    width = near_ref.shape[1]
    half = width // 2

    def diag(ref):
        return jnp.concatenate([ref[0, :, :half], ref[1, :, :half]], axis=1)

    def edge(ref):
        return jnp.concatenate([ref[0, :, half:], ref[1, :, half:]], axis=1)

    grams = [(diag(own_ref), edge(own_ref), diag(p1_ref)), (diag(p3_ref), edge(p3_ref), diag(p2_ref))]
    bases = [(t.astype(BF), b.astype(BF)) for t, b in solve(grams, identity(width))]
    for i, ref in enumerate((near_ref, far_ref)):
        t, b = bases[i]
        ref[:width] = t
        ref[width:] = b
        g = [split(x) for x in grams[i]]
        up = half_mul(g[0], t) + half_mul(g[1], b)
        down = half_mul(g[1], t, dot_t) + half_mul(g[2], b)
        outer_ref[i] = half_mul_t(t, split(up)) + half_mul_t(b, split(down))


def level0(place, parts, width):
    half = width // 2
    return pl.pallas_call(
        level0_kernel,
        out_shape=[
            jax.ShapeDtypeStruct((2 * width, width), BF),
            jax.ShapeDtypeStruct((2 * width, width), BF),
            jax.ShapeDtypeStruct((2, width, width), F32),
        ],
        in_specs=[pl.BlockSpec(memory_space=pltpu.SMEM)] + [pl.BlockSpec(memory_space=pl.ANY)] * 8,
        scratch_shapes=[
            pltpu.VMEM((2, width, width), F32),
            pltpu.VMEM((2, width, half), F32),
            pltpu.VMEM((2, width, half), F32),
            pltpu.VMEM((2, width, width), F32),
            pltpu.SemaphoreType.DMA((8,)),
        ],
        compiler_params=pltpu.CompilerParams(vmem_limit_bytes=40 * 2**20),
        cost_estimate=pl.CostEstimate(flops=12 * 10**9, bytes_accessed=2 * 2**20, transcendentals=0),
        name="level0",
    )(place, *parts)


def level1_kernel(place_ref, near_ref, far_ref, outer_ref, c0_ref, c1_ref, c2_ref, c3_ref, last_ref, between_ref):
    run = place_ref[0]
    width = near_ref.shape[1]
    near = (near_ref[:width], near_ref[width:])
    far = (far_ref[width:], far_ref[:width])

    def between(first, second, f0, f1, s0, s1):
        (ft, fb), (st, sb) = first, second
        to_s1, to_s0, from_s0, from_s1 = (split(x[...]) for x in (f0, f1, s0, s1))
        up = half_mul(to_s1, sb) + half_mul(from_s1, st, dot_t)
        down = half_mul(to_s0, st) + half_mul(from_s0, sb, dot_t)
        return half_mul_t(ft, split(up)) + half_mul_t(fb, split(down))

    @pl.when(run < 2)
    def _():
        between_ref[...] = between(near, far, c0_ref, c1_ref, c2_ref, c3_ref)

    @pl.when(run >= 2)
    def _():
        between_ref[...] = between(far, near, c2_ref, c3_ref, c0_ref, c1_ref).T

    [(t, b)] = solve([(outer_ref[0], between_ref[...], outer_ref[1])], identity(width))
    lanes = last_ref.shape[1]
    quarter = lanes // 2
    pick_row = lax.broadcasted_iota(jnp.int32, (width, lanes), 0)
    pick_col = lax.broadcasted_iota(jnp.int32, (width, lanes), 1)
    pick_col = jnp.where(pick_col >= quarter, pick_col - quarter, pick_col)
    pick = (pick_row == pick_col + run * quarter).astype(F32).astype(BF)
    last_ref[:width] = dot(t.astype(BF), pick).astype(BF)
    last_ref[width:] = dot(b.astype(BF), pick).astype(BF)


def level1(place, near, far, outer, crosses, width):
    return pl.pallas_call(
        level1_kernel,
        out_shape=jax.ShapeDtypeStruct((2 * width, width // 2), BF),
        in_specs=[pl.BlockSpec(memory_space=pltpu.SMEM)] + [pl.BlockSpec(memory_space=pltpu.VMEM)] * 7,
        out_specs=pl.BlockSpec(memory_space=pltpu.VMEM),
        scratch_shapes=[pltpu.VMEM((width, width), F32)],
        compiler_params=pltpu.CompilerParams(vmem_limit_bytes=40 * 2**20),
        cost_estimate=pl.CostEstimate(flops=8 * 10**9, bytes_accessed=2 * 2**20, transcendentals=0),
        name="level1",
    )(place, near, far, outer, *crosses)


def pack_kernel(shards, slots, counts_ref, own_ref, p1_ref, p2a_ref, p2b_ref, p3_ref, near_ref, far_ref, last_ref,
                out_ref, rows_ref, slot_ref):
    width = own_ref.shape[1]
    cells = own_ref.shape[0]
    tile = 512
    for k in range(cells // tile):
        at = pl.ds(k * tile, tile)
        half = cells // 2
        p2 = p2a_ref[at] if k * tile < half else p2b_ref[pl.ds(k * tile - half, tile)]
        near = (dot(own_ref[at], near_ref[:width]) + dot(p1_ref[at], near_ref[width:])).astype(BF)
        far = (dot(p3_ref[at], far_ref[:width]) + dot(p2, far_ref[width:])).astype(BF)
        rows_ref[at] = dot(near, last_ref[:width]) + dot(far, last_ref[width:])
    pad = rows_ref.shape[0] - cells
    rows_ref[pl.ds(cells, pad)] = jnp.zeros((pad, rows_ref.shape[1]), F32)
    half_slot = slots // 2
    lane = lax.broadcasted_iota(jnp.int32, (half_slot, rows_ref.shape[1]), 1)

    def one(d, start):
        first = rows_ref[pl.ds(start, half_slot)]
        second = rows_ref[pl.ds(start + half_slot, half_slot)]
        slot_ref[pl.ds(pl.multiple_of(d * half_slot, 8), half_slot)] = jnp.where(
            lane < rows_ref.shape[1] // 2, first, second
        )
        return jnp.minimum(start + counts_ref[d], cells)

    lax.fori_loop(0, shards, one, jnp.int32(0))
    out_ref[...] = slot_ref[...].astype(BF)


def unpack_kernel(shards, slots, counts_ref, in_ref, out_ref, slot_ref, rows_ref):
    cells, quarter = out_ref.shape
    half_slot = slots // 2
    slot_ref[...] = in_ref[...].astype(F32)

    def one(s, start):
        pair = slot_ref[pl.ds(pl.multiple_of(s * half_slot, 8), half_slot)]
        rows_ref[pl.ds(start, half_slot)] = pair
        rows_ref[pl.ds(start + half_slot, half_slot)] = pltpu.roll(pair, quarter, 1)
        return jnp.minimum(start + counts_ref[s], cells)

    lax.fori_loop(0, shards, one, jnp.int32(0))
    out_ref[...] = rows_ref[pl.ds(0, cells), :quarter].astype(BF)


def body(snapshots, run_counts, route_counts):
    cells, width = snapshots.shape
    shards = lax.axis_size("space")
    runs = lax.axis_size("run")
    slots = 3 * cells // (2 * shards)
    run = lax.axis_index("run")
    spot = lax.axis_index("space")
    core = lax.rem(spot, 2)
    groups = [[2 * i + c for i in range(shards // 2)] for c in range(2)]

    def across(x, mask):
        return lax.ppermute(x, "run", [(r, r ^ mask) for r in range(runs)])

    def other_core(x):
        return lax.ppermute(x, "space", [(s, s ^ 1) for s in range(shards)])

    def opposite(p1, p3):
        half = p1.shape[0] // 2
        return across(p1[:half], 3), across(p3[half:], 1)

    keep = jnp.arange(width, dtype=jnp.int32) < run_counts[0]
    own = jnp.where(keep[None, :], snapshots, jnp.zeros((), BF))
    p1, p3 = across(own, 1), across(own, 3)

    left = jnp.where(run < 2, own, p1)
    blocks = [dot_t(own, own), dot_t(own, p1), dot_t(left, p3)]
    half = width // 2

    def side(first):
        return jnp.concatenate([jnp.where(first, b[:, :half], b[:, half:]) for b in blocks], axis=1)

    mine = side(core == 0) + other_core(side(core == 1))
    cut = mine.shape[1]
    pieces = mine.reshape(shards // 2, -1, cut)
    pieces = lax.all_to_all(pieces, "space", 0, 0, tiled=True, axis_index_groups=groups)
    total = jnp.sum(pieces, axis=0)
    pieces = lax.all_to_all(
        jnp.broadcast_to(total, pieces.shape), "space", 0, 0, tiled=True, axis_index_groups=groups
    )
    spread = pieces.reshape(width, cut)
    g0, c0 = spread[:, :width], spread[:, width:]
    g1, g3 = across(g0[:, :half], 1), across(g0, 3)
    g2 = across(g3[:, :half], 1)
    c0b = other_core(c0)
    c0 = jnp.where(core == 0, jnp.concatenate([c0, c0b], axis=1), jnp.concatenate([c0b, c0], axis=1))
    parts = []
    for g in (g0, g1, g2, g3):
        parts += [g, other_core(g)]
    g2, c0, q1, q3 = lax.optimization_barrier((g2, c0, p1, p3))
    parts[4] = g2
    crosses = [c0, across(c0, 1), across(c0, 2), across(c0, 3)]
    p2a, p2b = opposite(q1, q3)
    place = jnp.stack([run, core]).astype(jnp.int32)
    near, far, outer = level0(place, parts, width)
    last = level1(place, near, far, outer, crosses, width)

    send = lax.dynamic_index_in_dim(route_counts, spot, 0, keepdims=False)
    recv = lax.dynamic_index_in_dim(route_counts, spot, 1, keepdims=False)
    smem = pl.BlockSpec(memory_space=pltpu.SMEM)
    vmem = pl.BlockSpec(memory_space=pltpu.VMEM)
    lanes = width // 2
    flat = shards * slots // 2
    packed = pl.pallas_call(
        functools.partial(pack_kernel, shards, slots),
        out_shape=jax.ShapeDtypeStruct((flat, lanes), BF),
        in_specs=[smem] + [vmem] * 8,
        out_specs=vmem,
        scratch_shapes=[pltpu.VMEM((cells + 64, lanes), F32), pltpu.VMEM((flat, lanes), F32)],
        compiler_params=pltpu.CompilerParams(vmem_limit_bytes=40 * 2**20),
        name="rotate_and_pack",
    )(send, own, p1, p2a, p2b, p3, near, far, last)
    arrived = lax.all_to_all(packed.reshape(shards, slots // 2, lanes), "space", 0, 0, tiled=True)
    return pl.pallas_call(
        functools.partial(unpack_kernel, shards, slots),
        out_shape=jax.ShapeDtypeStruct((cells, width // runs), BF),
        in_specs=[smem, vmem],
        out_specs=vmem,
        scratch_shapes=[pltpu.VMEM((flat, lanes), F32), pltpu.VMEM((cells + 64, lanes), F32)],
        compiler_params=pltpu.CompilerParams(vmem_limit_bytes=40 * 2**20),
        name="unpack",
    )(recv, arrived.reshape(flat, lanes))


def solution(mesh):
    in_specs = (P("space", "run"), P("run"), P())
    out_specs = P("space", "run")
    return jax.shard_map(body, mesh=mesh, in_specs=in_specs, out_specs=out_specs, check_vma=False)
```

```python
import functools
import math

import jax
import jax.numpy as jnp
from jax import lax
from jax.experimental import pallas as pl
from jax.experimental.pallas import tpu as pltpu
from jax.sharding import PartitionSpec as P

ITERS = 2
NS_STEPS = 8
BF = jnp.bfloat16
F32 = jnp.float32


def dot(a, b):
    return lax.dot_general(a, b, (((1,), (0,)), ((), ())), preferred_element_type=F32)


def dot_t(a, b):
    return lax.dot_general(a, b, (((0,), (0,)), ((), ())), preferred_element_type=F32)


def split(x):
    hi = x.astype(BF)
    return hi, (x - hi.astype(F32)).astype(BF)


def mul(a, b, op=dot):
    return op(a[0], b[0]) + (op(a[0], b[1]) + op(a[1], b[0]))


def half_mul(a, b, op=dot):
    return op(a[0], b) + op(a[1], b)


def half_mul_t(b, a):
    return dot_t(b, a[0]) + dot_t(b, a[1])


def solve(grams, eye):
    root = 1.0 / math.sqrt(2.0)
    gs = [(split(a), split(b), split(c)) for a, b, c in grams]
    heads = [((a + b) * root, (b.T + c) * root) for a, b, c in grams]
    for sweep in range(ITERS):
        scaled = []
        for pt, pb in heads:
            norm = lax.rsqrt(jnp.sum(pt * pt + pb * pb, keepdims=True) + 1e-06)
            scaled.append((split(pt * norm), split(pb * norm)))
        moments = [mul(st, st, dot_t) + mul(sb, sb, dot_t) for st, sb in scaled]
        turns = None
        ahead, fill = [], []
        for (a, b, c), (st, sb) in zip(gs, scaled):
            cell = [None] * 4
            ahead.append(cell)
            for n, f in enumerate((lambda a=a, st=st: mul(a, st), lambda b=b, sb=sb: mul(b, sb),
                                   lambda b=b, st=st: mul(b, st, dot_t), lambda c=c, sb=sb: mul(c, sb))):
                fill.append((cell, n, f))
        if sweep + 1 == ITERS:
            fill = []
        for k in range(NS_STEPS):
            last = k == NS_STEPS - 1
            halves = [split(m) for m in moments]
            weights = [1.5 * eye - 0.5 * m for m in moments]
            if not last:
                squares = [mul(h, h) for h in halves]
            turns = weights if k == 0 else [mul(split(t), split(w)) for t, w in zip(turns, weights)]
            for cell, n, f in fill[:len(grams)]:
                cell[n] = f()
            fill = fill[len(grams):]
            if not last:
                moments = [mul(h, split(2.25 * eye - 1.5 * m + 0.25 * q)) for h, m, q in zip(halves, moments, squares)]
        turns = [split(t) for t in turns]
        if sweep + 1 < ITERS:
            scaled = [(split(c[0] + c[1]), split(c[2] + c[3])) for c in ahead]
        heads = [(mul(st, t), mul(sb, t)) for (st, sb), t in zip(scaled, turns)]
    return heads


def identity(width):
    rows = lax.broadcasted_iota(jnp.int32, (width, width), 0)
    return (rows == lax.broadcasted_iota(jnp.int32, (width, width), 1)).astype(F32)


def level0_kernel(place_ref, *refs):
    parts, (near_ref, far_ref, outer_ref, own_ref, rest_ref, sems) = refs[:4], refs[4:]
    core = place_ref[1]
    copies = []
    for j, ref in enumerate((own_ref, rest_ref)):
        for k, slot in enumerate((core, 1 - core)):
            copies.append(pltpu.make_async_copy(parts[2 * j + k], ref.at[slot], sems.at[2 * j + k]))
    for c in copies:
        c.start()
    for c in copies:
        c.wait()
    width = near_ref.shape[1]
    half = width // 2

    def block(ref, n):
        at = slice(n * half, (n + 1) * half)
        return jnp.concatenate([ref[0, :, at], ref[1, :, at]], axis=1)

    near = (block(own_ref, 0), block(own_ref, 1), block(rest_ref, 0))
    far = (block(rest_ref, 2), block(rest_ref, 3), block(rest_ref, 1))
    grams = [near, far]
    bases = [(t.astype(BF), b.astype(BF)) for t, b in solve(grams, identity(width))]
    for i, ref in enumerate((near_ref, far_ref)):
        t, b = bases[i]
        ref[:width] = t
        ref[width:] = b
        g = [split(x) for x in grams[i]]
        up = half_mul(g[0], t) + half_mul(g[1], b)
        down = half_mul(g[1], t, dot_t) + half_mul(g[2], b)
        outer_ref[i] = half_mul_t(t, split(up)) + half_mul_t(b, split(down))


def level0(place, parts, width):
    half = width // 2
    return pl.pallas_call(
        level0_kernel,
        out_shape=[
            jax.ShapeDtypeStruct((2 * width, width), BF),
            jax.ShapeDtypeStruct((2 * width, width), BF),
            jax.ShapeDtypeStruct((2, width, width), F32),
        ],
        in_specs=[pl.BlockSpec(memory_space=pltpu.SMEM)] + [pl.BlockSpec(memory_space=pl.ANY)] * 4,
        scratch_shapes=[
            pltpu.VMEM((2, width, 3 * half), F32),
            pltpu.VMEM((2, width, 4 * half), F32),
            pltpu.SemaphoreType.DMA((4,)),
        ],
        compiler_params=pltpu.CompilerParams(vmem_limit_bytes=40 * 2**20),
        cost_estimate=pl.CostEstimate(flops=12 * 10**9, bytes_accessed=2 * 2**20, transcendentals=0),
        name="level0",
    )(place, *parts)


def level1_kernel(place_ref, near_ref, far_ref, outer_ref, c0_ref, c1_ref, c2_ref, c3_ref, last_ref, between_ref):
    run = place_ref[0]
    width = near_ref.shape[1]
    near = (near_ref[:width], near_ref[width:])
    far = (far_ref[width:], far_ref[:width])

    def between(first, second, f0, f1, s0, s1):
        (ft, fb), (st, sb) = first, second
        to_s1, to_s0, from_s0, from_s1 = (split(x[...]) for x in (f0, f1, s0, s1))
        up = half_mul(to_s1, sb) + half_mul(from_s1, st, dot_t)
        down = half_mul(to_s0, st) + half_mul(from_s0, sb, dot_t)
        return half_mul_t(ft, split(up)) + half_mul_t(fb, split(down))

    @pl.when(run < 2)
    def _():
        between_ref[...] = between(near, far, c0_ref, c1_ref, c2_ref, c3_ref)

    @pl.when(run >= 2)
    def _():
        between_ref[...] = between(far, near, c2_ref, c3_ref, c0_ref, c1_ref).T

    [(t, b)] = solve([(outer_ref[0], between_ref[...], outer_ref[1])], identity(width))
    lanes = last_ref.shape[1]
    quarter = lanes // 2
    pick_row = lax.broadcasted_iota(jnp.int32, (width, lanes), 0)
    pick_col = lax.broadcasted_iota(jnp.int32, (width, lanes), 1)
    pick_col = jnp.where(pick_col >= quarter, pick_col - quarter, pick_col)
    pick = (pick_row == pick_col + run * quarter).astype(F32).astype(BF)
    last_ref[:width] = dot(t.astype(BF), pick).astype(BF)
    last_ref[width:] = dot(b.astype(BF), pick).astype(BF)


def level1(place, near, far, outer, crosses, width):
    return pl.pallas_call(
        level1_kernel,
        out_shape=jax.ShapeDtypeStruct((2 * width, width // 2), BF),
        in_specs=[pl.BlockSpec(memory_space=pltpu.SMEM)] + [pl.BlockSpec(memory_space=pltpu.VMEM)] * 7,
        out_specs=pl.BlockSpec(memory_space=pltpu.VMEM),
        scratch_shapes=[pltpu.VMEM((width, width), F32)],
        compiler_params=pltpu.CompilerParams(vmem_limit_bytes=40 * 2**20),
        cost_estimate=pl.CostEstimate(flops=8 * 10**9, bytes_accessed=2 * 2**20, transcendentals=0),
        name="level1",
    )(place, near, far, outer, *crosses)


def pack_kernel(shards, slots, valid_ref, counts_ref, rows_ref, own_ref, out_ref, wide_ref):
    cells = rows_ref.shape[0]
    strips, _, lanes = wide_ref.shape
    pad = wide_ref.shape[1] - cells
    for h in range(strips):
        at = slice(h * lanes, (h + 1) * lanes)
        keep = lax.broadcasted_iota(jnp.int32, (cells, lanes), 1) + h * lanes < valid_ref[0]
        rows = jnp.where(keep, rows_ref[:, at].astype(F32), 0.0)
        own_ref[:, at] = rows.astype(BF)
        wide_ref[h, pl.ds(0, cells)] = rows
        wide_ref[h, pl.ds(cells, pad)] = jnp.zeros((pad, lanes), F32)

    def one(d, start):
        at = pl.ds(pl.multiple_of(d * slots, 16), slots)
        for h in range(strips):
            out_ref[at, h * lanes:(h + 1) * lanes] = wide_ref[h, pl.ds(start, slots)].astype(BF)
        return jnp.minimum(start + counts_ref[d], cells)

    lax.fori_loop(0, shards, one, jnp.int32(0), unroll=4)


def unpack_kernel(shards, slots, counts_ref, in_ref, out_ref, wide_ref):
    cells = out_ref.shape[0]
    strips, _, lanes = wide_ref.shape

    def one(s, start):
        at = pl.ds(pl.multiple_of(s * slots, 16), slots)
        for h in range(strips):
            wide_ref[h, pl.ds(start, slots)] = in_ref[at, h * lanes:(h + 1) * lanes].astype(F32)
        return jnp.minimum(start + counts_ref[s], cells)

    lax.fori_loop(0, shards, one, jnp.int32(0), unroll=4)
    for h in range(strips):
        out_ref[:, h * lanes:(h + 1) * lanes] = wide_ref[h, pl.ds(0, cells)].astype(BF)


def rotate_kernel(own_ref, p1_ref, p2a_ref, p2b_ref, p3_ref, near_ref, far_ref, last_ref, out_ref):
    cells, width = own_ref.shape
    quarter = out_ref.shape[1]
    half = cells // 2
    tile = cells // 4
    for k in range(4):
        at = pl.ds(k * tile, tile)
        p2 = p2a_ref[at] if k * tile < half else p2b_ref[pl.ds(k * tile - half, tile)]
        near = (dot(own_ref[at], near_ref[:width]) + dot(p1_ref[at], near_ref[width:])).astype(BF)
        far = (dot(p3_ref[at], far_ref[:width]) + dot(p2, far_ref[width:])).astype(BF)
        both = dot(near, last_ref[:width]) + dot(far, last_ref[width:])
        out_ref[at] = both[:, :quarter].astype(BF)


def local_call(kernel, shapes, specs, scratch, name):
    outs = [jax.ShapeDtypeStruct(shape, BF) for shape in shapes]
    return pl.pallas_call(
        kernel,
        out_shape=outs,
        in_specs=[pl.BlockSpec(memory_space=m) for m in specs],
        out_specs=[pl.BlockSpec(memory_space=pltpu.VMEM) for _ in outs],
        scratch_shapes=scratch,
        compiler_params=pltpu.CompilerParams(vmem_limit_bytes=40 * 2**20),
        name=name,
    )


def body(snapshots, run_counts, route_counts):
    cells, width = snapshots.shape
    shards = lax.axis_size("space")
    runs = lax.axis_size("run")
    slots = 3 * cells // (2 * shards)
    run = lax.axis_index("run")
    spot = lax.axis_index("space")
    core = lax.rem(spot, 2)
    groups = [[2 * i + c for i in range(shards // 2)] for c in range(2)]

    def across(x, mask):
        return lax.ppermute(x, "run", [(r, r ^ mask) for r in range(runs)])

    def other_core(x):
        return lax.ppermute(x, "space", [(s, s ^ 1) for s in range(shards)])

    def opposite(p1, p3):
        half = p1.shape[0] // 2
        return across(p1[:half], 3), across(p3[half:], 1)

    send = lax.dynamic_index_in_dim(route_counts, spot, 0, keepdims=False)
    recv = lax.dynamic_index_in_dim(route_counts, spot, 1, keepdims=False)
    smem, vmem = pltpu.SMEM, pltpu.VMEM
    wide = [pltpu.VMEM((width // 128, cells + 64, 128), F32)]
    own, packed = local_call(
        functools.partial(pack_kernel, shards, slots),
        [(cells, width), (shards * slots, width)], [smem, smem, vmem], wide, "mask_and_pack",
    )(run_counts, send, snapshots)
    p1, p3 = across(own, 1), across(own, 3)
    arrived = lax.all_to_all(packed.reshape(shards, slots, width), "space", 0, 0, tiled=True)

    left = jnp.where(run < 2, own, p1)
    blocks = [dot_t(own, own), dot_t(own, p1), dot_t(left, p3)]
    half = width // 2

    def side(first):
        return jnp.concatenate([jnp.where(first, b[:, :half], b[:, half:]) for b in blocks], axis=1)

    mine = side(core == 0) + other_core(side(core == 1))
    mine, arrived = lax.optimization_barrier((mine, arrived))
    cut = mine.shape[1]
    [routed] = local_call(functools.partial(unpack_kernel, shards, slots), [(cells, width)], [smem, vmem], wide, "unpack")(
        recv, arrived.reshape(shards * slots, width)
    )
    pieces = mine.reshape(shards // 2, -1, cut)
    pieces = lax.all_to_all(pieces, "space", 0, 0, tiled=True, axis_index_groups=groups)
    pieces, routed = lax.optimization_barrier((pieces, routed))
    r1, r3 = across(routed, 1), across(routed, 3)
    r2a, r2b = opposite(r1, r3)
    total = jnp.sum(pieces, axis=0)
    pieces = lax.all_to_all(
        jnp.broadcast_to(total, pieces.shape), "space", 0, 0, tiled=True, axis_index_groups=groups
    )
    spread = pieces.reshape(width, cut)
    g3 = across(spread[:, :width], 3)
    g1 = across(spread[:, :half], 1)
    swap = other_core(spread)
    g2 = across(g3[:, :half], 1)
    c0 = jnp.where(
        core == 0,
        jnp.concatenate([spread[:, width:], swap[:, width:]], axis=1),
        jnp.concatenate([swap[:, width:], spread[:, width:]], axis=1),
    )
    crosses = [c0, across(c0, 1), across(c0, 2), across(c0, 3)]
    mine = jnp.concatenate([g1, g2, g3], axis=1)
    place = jnp.stack([run, core]).astype(jnp.int32)
    near, far, outer = level0(place, [spread, swap, mine, other_core(mine)], width)
    last = level1(place, near, far, outer, crosses, width)
    [modes] = local_call(rotate_kernel, [(cells, width // runs)], [vmem] * 8, [], "rotate")(
        routed, r1, r2a, r2b, r3, near, far, last
    )
    return modes


def solution(mesh):
    in_specs = (P("space", "run"), P("run"), P())
    out_specs = P("space", "run")
    return jax.shard_map(body, mesh=mesh, in_specs=in_specs, out_specs=out_specs, check_vma=False)
```

```python
import functools
import math

import jax
import jax.numpy as jnp
from jax import lax
from jax.experimental import pallas as pl
from jax.experimental.pallas import tpu as pltpu
from jax.sharding import PartitionSpec as P

ITERS = 2
NS_STEPS = 8
BF = jnp.bfloat16
F32 = jnp.float32


def dot(a, b):
    return lax.dot_general(a, b, (((1,), (0,)), ((), ())), preferred_element_type=F32)


def dot_t(a, b):
    return lax.dot_general(a, b, (((0,), (0,)), ((), ())), preferred_element_type=F32)


def split(x):
    hi = x.astype(BF)
    return hi, (x - hi.astype(F32)).astype(BF)


def mul(a, b, op=dot):
    return op(a[0], b[0]) + (op(a[0], b[1]) + op(a[1], b[0]))


def half_mul(a, b, op=dot):
    return op(a[0], b) + op(a[1], b)


def half_mul_t(b, a):
    return dot_t(b, a[0]) + dot_t(b, a[1])


def solve(grams, eye):
    root = 1.0 / math.sqrt(2.0)
    gs = [(split(a), split(b), split(c)) for a, b, c in grams]
    heads = [((a + b) * root, (b.T + c) * root) for a, b, c in grams]
    for sweep in range(ITERS):
        scaled = []
        for pt, pb in heads:
            norm = lax.rsqrt(jnp.sum(pt * pt + pb * pb, keepdims=True) + 1e-06)
            scaled.append((split(pt * norm), split(pb * norm)))
        moments = [mul(st, st, dot_t) + mul(sb, sb, dot_t) for st, sb in scaled]
        turns = None
        ahead, fill = [], []
        for (a, b, c), (st, sb) in zip(gs, scaled):
            cell = [None] * 4
            ahead.append(cell)
            for n, f in enumerate((lambda a=a, st=st: mul(a, st), lambda b=b, sb=sb: mul(b, sb),
                                   lambda b=b, st=st: mul(b, st, dot_t), lambda c=c, sb=sb: mul(c, sb))):
                fill.append((cell, n, f))
        if sweep + 1 == ITERS:
            fill = []
        for k in range(NS_STEPS):
            last = k == NS_STEPS - 1
            halves = [split(m) for m in moments]
            weights = [1.5 * eye - 0.5 * m for m in moments]
            if not last:
                squares = [mul(h, h) for h in halves]
            turns = weights if k == 0 else [mul(split(t), split(w)) for t, w in zip(turns, weights)]
            for cell, n, f in fill[:len(grams)]:
                cell[n] = f()
            fill = fill[len(grams):]
            if not last:
                moments = [mul(h, split(2.25 * eye - 1.5 * m + 0.25 * q)) for h, m, q in zip(halves, moments, squares)]
        turns = [split(t) for t in turns]
        if sweep + 1 < ITERS:
            scaled = [(split(c[0] + c[1]), split(c[2] + c[3])) for c in ahead]
        heads = [(mul(st, t), mul(sb, t)) for (st, sb), t in zip(scaled, turns)]
    return heads


def identity(width):
    rows = lax.broadcasted_iota(jnp.int32, (width, width), 0)
    return (rows == lax.broadcasted_iota(jnp.int32, (width, width), 1)).astype(F32)


def level0_kernel(place_ref, *refs):
    parts, (near_ref, far_ref, outer_ref, own_ref, rest_ref, sems) = refs[:4], refs[4:]
    core = place_ref[1]
    copies = []
    for j, ref in enumerate((own_ref, rest_ref)):
        for k, slot in enumerate((core, 1 - core)):
            copies.append(pltpu.make_async_copy(parts[2 * j + k], ref.at[slot], sems.at[2 * j + k]))
    for c in copies:
        c.start()
    for c in copies:
        c.wait()
    width = near_ref.shape[1]
    half = width // 2

    def block(ref, n):
        at = slice(n * half, (n + 1) * half)
        return jnp.concatenate([ref[0, :, at], ref[1, :, at]], axis=1)

    near = (block(own_ref, 0), block(own_ref, 1), block(rest_ref, 0))
    far = (block(rest_ref, 2), block(rest_ref, 3), block(rest_ref, 1))
    grams = [near, far]
    bases = [(t.astype(BF), b.astype(BF)) for t, b in solve(grams, identity(width))]
    for i, ref in enumerate((near_ref, far_ref)):
        t, b = bases[i]
        ref[:width] = t
        ref[width:] = b
        g = [split(x) for x in grams[i]]
        up = half_mul(g[0], t) + half_mul(g[1], b)
        down = half_mul(g[1], t, dot_t) + half_mul(g[2], b)
        outer_ref[i] = half_mul_t(t, split(up)) + half_mul_t(b, split(down))


def level0(place, parts, width):
    half = width // 2
    return pl.pallas_call(
        level0_kernel,
        out_shape=[
            jax.ShapeDtypeStruct((2 * width, width), BF),
            jax.ShapeDtypeStruct((2 * width, width), BF),
            jax.ShapeDtypeStruct((2, width, width), F32),
        ],
        in_specs=[pl.BlockSpec(memory_space=pltpu.SMEM)] + [pl.BlockSpec(memory_space=pl.ANY)] * 4,
        scratch_shapes=[
            pltpu.VMEM((2, width, 3 * half), F32),
            pltpu.VMEM((2, width, 4 * half), F32),
            pltpu.SemaphoreType.DMA((4,)),
        ],
        compiler_params=pltpu.CompilerParams(vmem_limit_bytes=40 * 2**20),
        cost_estimate=pl.CostEstimate(flops=12 * 10**9, bytes_accessed=2 * 2**20, transcendentals=0),
        name="level0",
    )(place, *parts)


def level1_kernel(place_ref, near_ref, far_ref, outer_ref, c0_ref, c1_ref, c2_ref, c3_ref, last_ref, between_ref):
    run = place_ref[0]
    width = near_ref.shape[1]
    near = (near_ref[:width], near_ref[width:])
    far = (far_ref[width:], far_ref[:width])

    def between(first, second, f0, f1, s0, s1):
        (ft, fb), (st, sb) = first, second
        to_s1, to_s0, from_s0, from_s1 = (split(x[...]) for x in (f0, f1, s0, s1))
        up = half_mul(to_s1, sb) + half_mul(from_s1, st, dot_t)
        down = half_mul(to_s0, st) + half_mul(from_s0, sb, dot_t)
        return half_mul_t(ft, split(up)) + half_mul_t(fb, split(down))

    @pl.when(run < 2)
    def _():
        between_ref[...] = between(near, far, c0_ref, c1_ref, c2_ref, c3_ref)

    @pl.when(run >= 2)
    def _():
        between_ref[...] = between(far, near, c2_ref, c3_ref, c0_ref, c1_ref).T

    [(t, b)] = solve([(outer_ref[0], between_ref[...], outer_ref[1])], identity(width))
    lanes = last_ref.shape[1]
    quarter = lanes // 2
    pick_row = lax.broadcasted_iota(jnp.int32, (width, lanes), 0)
    pick_col = lax.broadcasted_iota(jnp.int32, (width, lanes), 1)
    pick_col = jnp.where(pick_col >= quarter, pick_col - quarter, pick_col)
    pick = (pick_row == pick_col + run * quarter).astype(F32).astype(BF)
    last_ref[:width] = dot(t.astype(BF), pick).astype(BF)
    last_ref[width:] = dot(b.astype(BF), pick).astype(BF)


def level1(place, near, far, outer, crosses, width):
    return pl.pallas_call(
        level1_kernel,
        out_shape=jax.ShapeDtypeStruct((2 * width, width // 2), BF),
        in_specs=[pl.BlockSpec(memory_space=pltpu.SMEM)] + [pl.BlockSpec(memory_space=pltpu.VMEM)] * 7,
        out_specs=pl.BlockSpec(memory_space=pltpu.VMEM),
        scratch_shapes=[pltpu.VMEM((width, width), F32)],
        compiler_params=pltpu.CompilerParams(vmem_limit_bytes=40 * 2**20),
        cost_estimate=pl.CostEstimate(flops=8 * 10**9, bytes_accessed=2 * 2**20, transcendentals=0),
        name="level1",
    )(place, near, far, outer, *crosses)


def pack_kernel(shards, slots, counts_ref, rows_ref, out_ref, wide_ref):
    cells = rows_ref.shape[0]
    strips, _, lanes = wide_ref.shape
    pad = wide_ref.shape[1] - cells
    for h in range(strips):
        at = slice(h * lanes, (h + 1) * lanes)
        wide_ref[h, pl.ds(0, cells)] = rows_ref[:, at].astype(F32)
        wide_ref[h, pl.ds(cells, pad)] = jnp.zeros((pad, lanes), F32)

    def one(d, start):
        at = pl.ds(pl.multiple_of(d * slots, 16), slots)
        for h in range(strips):
            out_ref[at, h * lanes:(h + 1) * lanes] = wide_ref[h, pl.ds(start, slots)].astype(BF)
        return jnp.minimum(start + counts_ref[d], cells)

    lax.fori_loop(0, shards, one, jnp.int32(0), unroll=4)


def unpack_kernel(shards, slots, counts_ref, in_ref, out_ref, wide_ref):
    cells = out_ref.shape[0]
    strips, _, lanes = wide_ref.shape

    def one(s, start):
        at = pl.ds(pl.multiple_of(s * slots, 16), slots)
        for h in range(strips):
            wide_ref[h, pl.ds(start, slots)] = in_ref[at, h * lanes:(h + 1) * lanes].astype(F32)
        return jnp.minimum(start + counts_ref[s], cells)

    lax.fori_loop(0, shards, one, jnp.int32(0), unroll=4)
    for h in range(strips):
        out_ref[:, h * lanes:(h + 1) * lanes] = wide_ref[h, pl.ds(0, cells)].astype(BF)


def rotate_kernel(own_ref, p1_ref, p2a_ref, p2b_ref, p3_ref, near_ref, far_ref, last_ref, out_ref):
    cells, width = own_ref.shape
    quarter = out_ref.shape[1]
    half = cells // 2
    tile = cells // 4
    for k in range(4):
        at = pl.ds(k * tile, tile)
        p2 = p2a_ref[at] if k * tile < half else p2b_ref[pl.ds(k * tile - half, tile)]
        near = (dot(own_ref[at], near_ref[:width]) + dot(p1_ref[at], near_ref[width:])).astype(BF)
        far = (dot(p3_ref[at], far_ref[:width]) + dot(p2, far_ref[width:])).astype(BF)
        both = dot(near, last_ref[:width]) + dot(far, last_ref[width:])
        out_ref[at] = both[:, :quarter].astype(BF)


def local_call(kernel, shapes, specs, scratch, name):
    outs = [jax.ShapeDtypeStruct(shape, BF) for shape in shapes]
    return pl.pallas_call(
        kernel,
        out_shape=outs,
        in_specs=[pl.BlockSpec(memory_space=m) for m in specs],
        out_specs=[pl.BlockSpec(memory_space=pltpu.VMEM) for _ in outs],
        scratch_shapes=scratch,
        compiler_params=pltpu.CompilerParams(vmem_limit_bytes=40 * 2**20),
        name=name,
    )


def body(snapshots, run_counts, route_counts):
    cells, width = snapshots.shape
    shards = lax.axis_size("space")
    runs = lax.axis_size("run")
    slots = 3 * cells // (2 * shards)
    run = lax.axis_index("run")
    spot = lax.axis_index("space")
    core = lax.rem(spot, 2)
    groups = [[2 * i + c for i in range(shards // 2)] for c in range(2)]

    def across(x, mask):
        return lax.ppermute(x, "run", [(r, r ^ mask) for r in range(runs)])

    def other_core(x):
        return lax.ppermute(x, "space", [(s, s ^ 1) for s in range(shards)])

    def opposite(p1, p3):
        half = p1.shape[0] // 2
        return across(p1[:half], 3), across(p3[half:], 1)

    send = lax.dynamic_index_in_dim(route_counts, spot, 0, keepdims=False)
    recv = lax.dynamic_index_in_dim(route_counts, spot, 1, keepdims=False)
    smem, vmem = pltpu.SMEM, pltpu.VMEM
    wide = [pltpu.VMEM((width // 128, cells + 64, 128), F32)]
    keep = jnp.arange(width, dtype=jnp.int32) < run_counts[0]
    own = jnp.where(keep[None, :], snapshots, jnp.zeros((), BF))
    p1, p3 = across(own, 1), across(own, 3)
    [packed] = local_call(
        functools.partial(pack_kernel, shards, slots), [(shards * slots, width)], [smem, vmem], wide, "pack"
    )(send, own)
    arrived = lax.all_to_all(packed.reshape(shards, slots, width), "space", 0, 0, tiled=True)

    left = jnp.where(run < 2, own, p1)
    blocks = [dot_t(own, own), dot_t(own, p1), dot_t(left, p3)]
    half = width // 2

    def side(first):
        return jnp.concatenate([jnp.where(first, b[:, :half], b[:, half:]) for b in blocks], axis=1)

    mine = side(core == 0) + other_core(side(core == 1))
    mine, arrived = lax.optimization_barrier((mine, arrived))
    cut = mine.shape[1]
    [routed] = local_call(functools.partial(unpack_kernel, shards, slots), [(cells, width)], [smem, vmem], wide, "unpack")(
        recv, arrived.reshape(shards * slots, width)
    )
    pieces = mine.reshape(shards // 2, -1, cut)
    pieces = lax.all_to_all(pieces, "space", 0, 0, tiled=True, axis_index_groups=groups)
    r1, r3 = across(routed, 1), across(routed, 3)
    pieces, routed = lax.optimization_barrier((pieces, routed))
    total = jnp.sum(pieces, axis=0)
    pieces = lax.all_to_all(
        jnp.broadcast_to(total, pieces.shape), "space", 0, 0, tiled=True, axis_index_groups=groups
    )
    spread = pieces.reshape(width, cut)
    spread, r1, r3 = lax.optimization_barrier((spread, r1, r3))
    g3 = across(spread[:, :width], 3)
    g1 = across(spread[:, :half], 1)
    swap = other_core(spread)
    g2 = across(spread[:, :half], 2)
    c0 = jnp.where(
        core == 0,
        jnp.concatenate([spread[:, width:], swap[:, width:]], axis=1),
        jnp.concatenate([swap[:, width:], spread[:, width:]], axis=1),
    )
    crosses = [c0, across(c0, 1), across(c0, 2), across(c0, 3)]
    mine = jnp.concatenate([g1, g2, g3], axis=1)
    place = jnp.stack([run, core]).astype(jnp.int32)
    near, far, outer = level0(place, [spread, swap, mine, other_core(mine)], width)
    near, q1, q3 = lax.optimization_barrier((near, r1, r3))
    r2a, r2b = opposite(q1, q3)
    last = level1(place, near, far, outer, crosses, width)
    [modes] = local_call(rotate_kernel, [(cells, width // runs)], [vmem] * 8, [], "rotate")(
        routed, r1, r2a, r2b, r3, near, far, last
    )
    return modes


def solution(mesh):
    in_specs = (P("space", "run"), P("run"), P())
    out_specs = P("space", "run")
    return jax.shard_map(body, mesh=mesh, in_specs=in_specs, out_specs=out_specs, check_vma=False)
```

```python
import functools
import math

import jax
import jax.numpy as jnp
from jax import lax
from jax.experimental import pallas as pl
from jax.experimental.pallas import tpu as pltpu
from jax.sharding import PartitionSpec as P

ITERS = 2
NS_STEPS = 8
BF = jnp.bfloat16
F32 = jnp.float32


def dot(a, b):
    return lax.dot_general(a, b, (((1,), (0,)), ((), ())), preferred_element_type=F32)


def dot_t(a, b):
    return lax.dot_general(a, b, (((0,), (0,)), ((), ())), preferred_element_type=F32)


def dot_nt(a, b):
    return lax.dot_general(a, b, (((1,), (1,)), ((), ())), preferred_element_type=F32)


def split(x):
    hi = x.astype(BF)
    return hi, (x - hi.astype(F32)).astype(BF)


def mul(a, b, op=dot):
    return op(a[0], b[0]) + (op(a[0], b[1]) + op(a[1], b[0]))


def half_mul(a, b, op=dot):
    return op(a[0], b) + op(a[1], b)


def half_mul_t(b, a):
    return dot_t(b, a[0]) + dot_t(b, a[1])


def solve(grams, eye):
    root = 1.0 / math.sqrt(2.0)
    gs = [(split(a), split(b), split(c)) for a, b, c in grams]
    heads = [((a + b) * root, (b.T + c) * root) for a, b, c in grams]
    for sweep in range(ITERS):
        scaled = []
        for pt, pb in heads:
            norm = lax.rsqrt(jnp.sum(pt * pt + pb * pb, keepdims=True) + 1e-06)
            scaled.append((split(pt * norm), split(pb * norm)))
        moments = [mul(st, st, dot_t) + mul(sb, sb, dot_t) for st, sb in scaled]
        turns = None
        ahead, fill = [], []
        for (a, b, c), (st, sb) in zip(gs, scaled):
            cell = [None] * 4
            ahead.append(cell)
            for n, f in enumerate((lambda a=a, st=st: mul(a, st), lambda b=b, sb=sb: mul(b, sb),
                                   lambda b=b, st=st: mul(b, st, dot_t), lambda c=c, sb=sb: mul(c, sb))):
                fill.append((cell, n, f))
        if sweep + 1 == ITERS:
            fill = []
        for k in range(NS_STEPS):
            last = k == NS_STEPS - 1
            halves = [split(m) for m in moments]
            weights = [1.5 * eye - 0.5 * m for m in moments]
            if not last:
                squares = [mul(h, h) for h in halves]
            turns = weights if k == 0 else [mul(split(t), split(w)) for t, w in zip(turns, weights)]
            for cell, n, f in fill[:len(grams)]:
                cell[n] = f()
            fill = fill[len(grams):]
            if not last:
                moments = [mul(h, split(2.25 * eye - 1.5 * m + 0.25 * q)) for h, m, q in zip(halves, moments, squares)]
        turns = [split(t) for t in turns]
        if sweep + 1 < ITERS:
            scaled = [(split(c[0] + c[1]), split(c[2] + c[3])) for c in ahead]
        heads = [(mul(st, t), mul(sb, t)) for (st, sb), t in zip(scaled, turns)]
    return heads


def identity(width):
    rows = lax.broadcasted_iota(jnp.int32, (width, width), 0)
    return (rows == lax.broadcasted_iota(jnp.int32, (width, width), 1)).astype(F32)


def level0_kernel(place_ref, *refs):
    parts, (near_ref, far_ref, outer_ref, own_ref, rest_ref, sems) = refs[:4], refs[4:]
    core = place_ref[1]
    copies = []
    for j, ref in enumerate((own_ref, rest_ref)):
        for k, slot in enumerate((core, 1 - core)):
            copies.append(pltpu.make_async_copy(parts[2 * j + k], ref.at[slot], sems.at[2 * j + k]))
    for c in copies:
        c.start()
    for c in copies:
        c.wait()
    width = near_ref.shape[1]
    half = width // 2

    def block(ref, n):
        at = slice(n * half, (n + 1) * half)
        return jnp.concatenate([ref[0, :, at], ref[1, :, at]], axis=1)

    near = (block(own_ref, 0), block(own_ref, 1), block(rest_ref, 0))
    far = (block(rest_ref, 2), block(rest_ref, 3), block(rest_ref, 1))
    grams = [near, far]
    bases = [(t.astype(BF), b.astype(BF)) for t, b in solve(grams, identity(width))]
    for i, ref in enumerate((near_ref, far_ref)):
        t, b = bases[i]
        ref[:width] = t
        ref[width:] = b
        g = [split(x) for x in grams[i]]
        up = half_mul(g[0], t) + half_mul(g[1], b)
        down = half_mul(g[1], t, dot_t) + half_mul(g[2], b)
        outer_ref[i] = half_mul_t(t, split(up)) + half_mul_t(b, split(down))


def level0(place, parts, width):
    half = width // 2
    return pl.pallas_call(
        level0_kernel,
        out_shape=[
            jax.ShapeDtypeStruct((2 * width, width), BF),
            jax.ShapeDtypeStruct((2 * width, width), BF),
            jax.ShapeDtypeStruct((2, width, width), F32),
        ],
        in_specs=[pl.BlockSpec(memory_space=pltpu.SMEM)] + [pl.BlockSpec(memory_space=pl.ANY)] * 4,
        scratch_shapes=[
            pltpu.VMEM((2, width, 3 * half), F32),
            pltpu.VMEM((2, width, 4 * half), F32),
            pltpu.SemaphoreType.DMA((4,)),
        ],
        compiler_params=pltpu.CompilerParams(vmem_limit_bytes=40 * 2**20),
        cost_estimate=pl.CostEstimate(flops=12 * 10**9, bytes_accessed=2 * 2**20, transcendentals=0),
        name="level0",
    )(place, *parts)


def level1_kernel(place_ref, near_ref, far_ref, outer_ref, c0_ref, c1_ref, c2_ref, c3_ref, last_ref, between_ref):
    run = place_ref[0]
    width = near_ref.shape[1]
    near = (near_ref[:width], near_ref[width:])
    far = (far_ref[width:], far_ref[:width])

    def between(first, second, f0, f1, s0, s1):
        (ft, fb), (st, sb) = first, second
        to_s1, to_s0, from_s0, from_s1 = (split(x[...]) for x in (f0, f1, s0, s1))
        up = half_mul(to_s1, sb) + half_mul(from_s1, st, dot_t)
        down = half_mul(to_s0, st) + half_mul(from_s0, sb, dot_t)
        return half_mul_t(ft, split(up)) + half_mul_t(fb, split(down))

    @pl.when(run < 2)
    def _():
        between_ref[...] = between(near, far, c0_ref, c1_ref, c2_ref, c3_ref)

    @pl.when(run >= 2)
    def _():
        between_ref[...] = between(far, near, c2_ref, c3_ref, c0_ref, c1_ref).T

    [(t, b)] = solve([(outer_ref[0], between_ref[...], outer_ref[1])], identity(width))
    quarter = last_ref.shape[0]
    pick_row = lax.broadcasted_iota(jnp.int32, (quarter, width), 0)
    pick_col = lax.broadcasted_iota(jnp.int32, (quarter, width), 1)
    pick = (pick_col == pick_row + run * quarter).astype(F32).astype(BF)
    last_ref[:, :width] = dot_nt(pick, t.astype(BF)).astype(BF)
    last_ref[:, width:] = dot_nt(pick, b.astype(BF)).astype(BF)


def level1(place, near, far, outer, crosses, width, quarter):
    return pl.pallas_call(
        level1_kernel,
        out_shape=jax.ShapeDtypeStruct((quarter, 2 * width), BF),
        in_specs=[pl.BlockSpec(memory_space=pltpu.SMEM)] + [pl.BlockSpec(memory_space=pltpu.VMEM)] * 7,
        out_specs=pl.BlockSpec(memory_space=pltpu.VMEM),
        scratch_shapes=[pltpu.VMEM((width, width), F32)],
        compiler_params=pltpu.CompilerParams(vmem_limit_bytes=40 * 2**20),
        cost_estimate=pl.CostEstimate(flops=8 * 10**9, bytes_accessed=2 * 2**20, transcendentals=0),
        name="level1",
    )(place, near, far, outer, *crosses)


def pack_kernel(shards, slots, counts_ref, rows_ref, out_ref, wide_ref):
    cells = rows_ref.shape[0]
    strips, _, lanes = wide_ref.shape
    pad = wide_ref.shape[1] - cells
    for h in range(strips):
        at = slice(h * lanes, (h + 1) * lanes)
        wide_ref[h, pl.ds(0, cells)] = rows_ref[:, at].astype(F32)
        wide_ref[h, pl.ds(cells, pad)] = jnp.zeros((pad, lanes), F32)

    def one(d, start):
        at = pl.ds(pl.multiple_of(d * slots, 16), slots)
        for h in range(strips):
            out_ref[at, h * lanes:(h + 1) * lanes] = wide_ref[h, pl.ds(start, slots)].astype(BF)
        return jnp.minimum(start + counts_ref[d], cells)

    lax.fori_loop(0, shards, one, jnp.int32(0), unroll=4)


def unpack_kernel(shards, slots, counts_ref, in_ref, out_ref, turned_ref, wide_ref):
    cells = out_ref.shape[0]
    half = cells // 2
    strips, _, lanes = wide_ref.shape

    def one(s, start):
        at = pl.ds(pl.multiple_of(s * slots, 16), slots)
        for h in range(strips):
            wide_ref[h, pl.ds(start, slots)] = in_ref[at, h * lanes:(h + 1) * lanes].astype(F32)
        return jnp.minimum(start + counts_ref[s], cells)

    lax.fori_loop(0, shards, one, jnp.int32(0), unroll=4)
    for h in range(strips):
        at = slice(h * lanes, (h + 1) * lanes)
        for k in range(2):
            rows = wide_ref[h, pl.ds(k * half, half)].astype(BF)
            out_ref[pl.ds(k * half, half), at] = rows
            turned_ref[pl.ds((1 - k) * half, half), at] = rows


def rotate_kernel(tiles, own, p1, p2a, p2b, p3, near_ref, far_ref, last_ref, out_ref):
    width = near_ref.shape[1]

    def turn(p2):
        near = (dot(own[...], near_ref[:width]) + dot(p1[...], near_ref[width:])).astype(BF)
        far = (dot(p3[...], far_ref[:width]) + dot(p2[...], far_ref[width:])).astype(BF)
        out_ref[...] = (dot_nt(last_ref[:, :width], near) + dot_nt(last_ref[:, width:], far)).astype(BF)

    @pl.when(pl.program_id(0) < tiles)
    def _():
        turn(p2a)

    @pl.when(pl.program_id(0) >= tiles)
    def _():
        turn(p2b)


def rotate(own, p1, p2a, p2b, p3, near, far, last):
    quarter = last.shape[0]
    tiles = 2
    cells, width = own.shape
    tile = cells // (2 * tiles)
    straight = pl.BlockSpec((tile, width), lambda i: (i, 0))
    low = pl.BlockSpec((tile, width), lambda i: (jnp.minimum(i, tiles - 1), 0))
    high = pl.BlockSpec((tile, width), lambda i: (jnp.maximum(i - tiles, 0), 0))
    swapped = pl.BlockSpec((tile, width), lambda i: (jnp.where(i < tiles, i + tiles, i - tiles), 0))
    whole = [pl.BlockSpec(x.shape, lambda i: (0, 0)) for x in (near, far, last)]
    return pl.pallas_call(
        functools.partial(rotate_kernel, tiles),
        grid=(2 * tiles,),
        out_shape=jax.ShapeDtypeStruct((quarter, cells), BF),
        in_specs=[straight, straight, low, high, swapped] + whole,
        out_specs=pl.BlockSpec((quarter, tile), lambda i: (0, i)),
        compiler_params=pltpu.CompilerParams(vmem_limit_bytes=40 * 2**20),
        name="rotate",
    )(own, p1, p2a, p2b, p3, near, far, last)


def local_call(kernel, shapes, specs, scratch, name):
    outs = [jax.ShapeDtypeStruct(shape, BF) for shape in shapes]
    return pl.pallas_call(
        kernel,
        out_shape=outs,
        in_specs=[pl.BlockSpec(memory_space=m) for m in specs],
        out_specs=[pl.BlockSpec(memory_space=pltpu.VMEM) for _ in outs],
        scratch_shapes=scratch,
        compiler_params=pltpu.CompilerParams(vmem_limit_bytes=40 * 2**20),
        name=name,
    )


def body(snapshots, run_counts, route_counts):
    cells, width = snapshots.shape
    shards = lax.axis_size("space")
    runs = lax.axis_size("run")
    slots = 3 * cells // (2 * shards)
    run = lax.axis_index("run")
    spot = lax.axis_index("space")
    core = lax.rem(spot, 2)
    groups = [[2 * i + c for i in range(shards // 2)] for c in range(2)]

    def across(x, mask):
        return lax.ppermute(x, "run", [(r, r ^ mask) for r in range(runs)])

    def other_core(x):
        return lax.ppermute(x, "space", [(s, s ^ 1) for s in range(shards)])

    send = lax.dynamic_index_in_dim(route_counts, spot, 0, keepdims=False)
    recv = lax.dynamic_index_in_dim(route_counts, spot, 1, keepdims=False)
    smem, vmem = pltpu.SMEM, pltpu.VMEM
    wide = [pltpu.VMEM((width // 128, cells + 64, 128), F32)]
    keep = jnp.arange(width, dtype=jnp.int32) < run_counts[0]
    own = jnp.where(keep[None, :], snapshots, jnp.zeros((), BF))
    p1, p3 = across(own, 1), across(own, 3)
    [packed] = local_call(
        functools.partial(pack_kernel, shards, slots), [(shards * slots, width)], [smem, vmem], wide, "pack"
    )(send, own)
    arrived = lax.all_to_all(packed.reshape(shards, slots, width), "space", 0, 0, tiled=True)

    left = jnp.where(run < 2, own, p1)
    blocks = [dot_t(own, own), dot_t(own, p1), dot_t(left, p3)]
    half = width // 2

    def side(first):
        return jnp.concatenate([jnp.where(first, b[:, :half], b[:, half:]) for b in blocks], axis=1)

    mine = side(core == 0) + other_core(side(core == 1))
    mine, arrived = lax.optimization_barrier((mine, arrived))
    cut = mine.shape[1]
    routed, turned = local_call(
        functools.partial(unpack_kernel, shards, slots), [(cells, width)] * 2, [smem, vmem], wide, "unpack"
    )(recv, arrived.reshape(shards * slots, width))
    pieces = mine.reshape(shards // 2, -1, cut)
    pieces = lax.all_to_all(pieces, "space", 0, 0, tiled=True, axis_index_groups=groups)
    r1, r3 = across(routed, 1), across(turned, 3)
    pieces, routed = lax.optimization_barrier((pieces, routed))
    total = jnp.sum(pieces, axis=0)
    pieces = lax.all_to_all(
        jnp.broadcast_to(total, pieces.shape), "space", 0, 0, tiled=True, axis_index_groups=groups
    )
    spread = pieces.reshape(width, cut)
    r2a, r2b = across(r1[:cells // 2], 3), across(r3[:cells // 2], 1)
    spread, r1, r3 = lax.optimization_barrier((spread, r1, r3))
    swap = other_core(spread)
    g3 = across(spread[:, :width], 3)
    g1 = across(spread[:, :half], 1)
    g2 = across(spread[:, :half], 2)
    c0 = jnp.where(
        core == 0,
        jnp.concatenate([spread[:, width:], swap[:, width:]], axis=1),
        jnp.concatenate([swap[:, width:], spread[:, width:]], axis=1),
    )
    g1, g2, g3, c0, swap, r2a, r2b = lax.optimization_barrier((g1, g2, g3, c0, swap, r2a, r2b))
    mine = jnp.concatenate([g1, g2, g3], axis=1)
    crosses = [c0, across(c0, 1), across(c0, 2), across(c0, 3)]
    place = jnp.stack([run, core]).astype(jnp.int32)
    near, far, outer = level0(place, [spread, swap, mine, other_core(mine)], width)
    last = level1(place, near, far, outer, crosses, width, width // runs)
    return rotate(routed, r1, r2a, r2b, r3, near, far, last).T


def solution(mesh):
    in_specs = (P("space", "run"), P("run"), P())
    out_specs = P("space", "run")
    return jax.shard_map(body, mesh=mesh, in_specs=in_specs, out_specs=out_specs, check_vma=False)
```

```python
import functools
import math

import jax
import jax.numpy as jnp
from jax import lax
from jax.experimental import pallas as pl
from jax.experimental.pallas import tpu as pltpu
from jax.sharding import PartitionSpec as P

ITERS = 2
NS_STEPS = 8
BF = jnp.bfloat16
F32 = jnp.float32


def dot(a, b):
    return lax.dot_general(a, b, (((1,), (0,)), ((), ())), preferred_element_type=F32)


def dot_t(a, b):
    return lax.dot_general(a, b, (((0,), (0,)), ((), ())), preferred_element_type=F32)


def dot_nt(a, b):
    return lax.dot_general(a, b, (((1,), (1,)), ((), ())), preferred_element_type=F32)


def split(x):
    hi = x.astype(BF)
    return hi, (x - hi.astype(F32)).astype(BF)


def mul(a, b, op=dot):
    return op(a[0], b[0]) + (op(a[0], b[1]) + op(a[1], b[0]))


def half_mul(a, b, op=dot):
    return op(a[0], b) + op(a[1], b)


def half_mul_t(b, a):
    return dot_t(b, a[0]) + dot_t(b, a[1])


def solve(grams, eye):
    root = 1.0 / math.sqrt(2.0)
    gs = [(split(a), split(b), split(c)) for a, b, c in grams]
    heads = [((a + b) * root, (b.T + c) * root) for a, b, c in grams]
    for sweep in range(ITERS):
        scaled = []
        for pt, pb in heads:
            norm = lax.rsqrt(jnp.sum(pt * pt + pb * pb, keepdims=True) + 1e-06)
            scaled.append((split(pt * norm), split(pb * norm)))
        moments = [mul(st, st, dot_t) + mul(sb, sb, dot_t) for st, sb in scaled]
        turns = None
        ahead, fill = [], []
        for (a, b, c), (st, sb) in zip(gs, scaled):
            cell = [None] * 4
            ahead.append(cell)
            for n, f in enumerate((lambda a=a, st=st: mul(a, st), lambda b=b, sb=sb: mul(b, sb),
                                   lambda b=b, st=st: mul(b, st, dot_t), lambda c=c, sb=sb: mul(c, sb))):
                fill.append((cell, n, f))
        if sweep + 1 == ITERS:
            fill = []
        for k in range(NS_STEPS):
            last = k == NS_STEPS - 1
            halves = [split(m) for m in moments]
            weights = [1.5 * eye - 0.5 * m for m in moments]
            if not last:
                squares = [mul(h, h) for h in halves]
            turns = weights if k == 0 else [mul(split(t), split(w)) for t, w in zip(turns, weights)]
            for cell, n, f in fill[:len(grams)]:
                cell[n] = f()
            fill = fill[len(grams):]
            if not last:
                moments = [mul(h, split(2.25 * eye - 1.5 * m + 0.25 * q)) for h, m, q in zip(halves, moments, squares)]
        turns = [split(t) for t in turns]
        if sweep + 1 < ITERS:
            scaled = [(split(c[0] + c[1]), split(c[2] + c[3])) for c in ahead]
        heads = [(mul(st, t), mul(sb, t)) for (st, sb), t in zip(scaled, turns)]
    return heads


def identity(width):
    rows = lax.broadcasted_iota(jnp.int32, (width, width), 0)
    return (rows == lax.broadcasted_iota(jnp.int32, (width, width), 1)).astype(F32)


def level0_kernel(place_ref, *refs):
    parts, (near_ref, far_ref, outer_ref, own_ref, rest_ref, sems) = refs[:4], refs[4:]
    core = place_ref[1]
    copies = []
    for j, ref in enumerate((own_ref, rest_ref)):
        for k, slot in enumerate((core, 1 - core)):
            copies.append(pltpu.make_async_copy(parts[2 * j + k], ref.at[slot], sems.at[2 * j + k]))
    for c in copies:
        c.start()
    for c in copies:
        c.wait()
    width = near_ref.shape[1]
    half = width // 2

    def block(ref, n):
        at = slice(n * half, (n + 1) * half)
        return jnp.concatenate([ref[0, :, at], ref[1, :, at]], axis=1)

    near = (block(own_ref, 0), block(own_ref, 1), block(rest_ref, 0))
    far = (block(rest_ref, 2), block(rest_ref, 3), block(rest_ref, 1))
    grams = [near, far]
    bases = [(t.astype(BF), b.astype(BF)) for t, b in solve(grams, identity(width))]
    for i, ref in enumerate((near_ref, far_ref)):
        t, b = bases[i]
        ref[:width] = t
        ref[width:] = b
        g = [split(x) for x in grams[i]]
        up = half_mul(g[0], t) + half_mul(g[1], b)
        down = half_mul(g[1], t, dot_t) + half_mul(g[2], b)
        outer_ref[i] = half_mul_t(t, split(up)) + half_mul_t(b, split(down))


def level0(place, parts, width):
    half = width // 2
    return pl.pallas_call(
        level0_kernel,
        out_shape=[
            jax.ShapeDtypeStruct((2 * width, width), BF),
            jax.ShapeDtypeStruct((2 * width, width), BF),
            jax.ShapeDtypeStruct((2, width, width), F32),
        ],
        in_specs=[pl.BlockSpec(memory_space=pltpu.SMEM)] + [pl.BlockSpec(memory_space=pl.ANY)] * 4,
        scratch_shapes=[
            pltpu.VMEM((2, width, 3 * half), F32),
            pltpu.VMEM((2, width, 4 * half), F32),
            pltpu.SemaphoreType.DMA((4,)),
        ],
        compiler_params=pltpu.CompilerParams(vmem_limit_bytes=40 * 2**20),
        cost_estimate=pl.CostEstimate(flops=12 * 10**9, bytes_accessed=2 * 2**20, transcendentals=0),
        name="level0",
    )(place, *parts)


def level1_kernel(place_ref, near_ref, far_ref, outer_ref, c0_ref, c1_ref, c2_ref, c3_ref, last_ref, between_ref):
    run = place_ref[0]
    width = near_ref.shape[1]
    near = (near_ref[:width], near_ref[width:])
    far = (far_ref[width:], far_ref[:width])

    def between(first, second, f0, f1, s0, s1):
        (ft, fb), (st, sb) = first, second
        to_s1, to_s0, from_s0, from_s1 = (split(x[...]) for x in (f0, f1, s0, s1))
        up = half_mul(to_s1, sb) + half_mul(from_s1, st, dot_t)
        down = half_mul(to_s0, st) + half_mul(from_s0, sb, dot_t)
        return half_mul_t(ft, split(up)) + half_mul_t(fb, split(down))

    @pl.when(run < 2)
    def _():
        between_ref[...] = between(near, far, c0_ref, c1_ref, c2_ref, c3_ref)

    @pl.when(run >= 2)
    def _():
        between_ref[...] = between(far, near, c2_ref, c3_ref, c0_ref, c1_ref).T

    [(t, b)] = solve([(outer_ref[0], between_ref[...], outer_ref[1])], identity(width))
    quarter = last_ref.shape[0]
    pick_row = lax.broadcasted_iota(jnp.int32, (quarter, width), 0)
    pick_col = lax.broadcasted_iota(jnp.int32, (quarter, width), 1)
    pick = (pick_col == pick_row + run * quarter).astype(F32).astype(BF)
    last_ref[:, :width] = dot_nt(pick, t.astype(BF)).astype(BF)
    last_ref[:, width:] = dot_nt(pick, b.astype(BF)).astype(BF)


def level1(place, near, far, outer, crosses, width, quarter):
    return pl.pallas_call(
        level1_kernel,
        out_shape=jax.ShapeDtypeStruct((quarter, 2 * width), BF),
        in_specs=[pl.BlockSpec(memory_space=pltpu.SMEM)] + [pl.BlockSpec(memory_space=pltpu.VMEM)] * 7,
        out_specs=pl.BlockSpec(memory_space=pltpu.VMEM),
        scratch_shapes=[pltpu.VMEM((width, width), F32)],
        compiler_params=pltpu.CompilerParams(vmem_limit_bytes=40 * 2**20),
        cost_estimate=pl.CostEstimate(flops=8 * 10**9, bytes_accessed=2 * 2**20, transcendentals=0),
        name="level1",
    )(place, near, far, outer, *crosses)


def pack_kernel(shards, slots, counts_ref, rows_ref, out_ref, wide_ref):
    cells = rows_ref.shape[0]
    strips, _, lanes = wide_ref.shape
    pad = wide_ref.shape[1] - cells
    for h in range(strips):
        at = slice(h * lanes, (h + 1) * lanes)
        wide_ref[h, pl.ds(0, cells)] = rows_ref[:, at].astype(F32)
        wide_ref[h, pl.ds(cells, pad)] = jnp.zeros((pad, lanes), F32)

    def one(d, start):
        at = pl.ds(pl.multiple_of(d * slots, 16), slots)
        for h in range(strips):
            out_ref[at, h * lanes:(h + 1) * lanes] = wide_ref[h, pl.ds(start, slots)].astype(BF)
        return jnp.minimum(start + counts_ref[d], cells)

    lax.fori_loop(0, shards, one, jnp.int32(0), unroll=4)


def unpack_kernel(shards, slots, counts_ref, in_ref, out_ref, turned_ref, wide_ref):
    cells = out_ref.shape[0]
    half = cells // 2
    strips, _, lanes = wide_ref.shape

    def one(s, start):
        at = pl.ds(pl.multiple_of(s * slots, 16), slots)
        for h in range(strips):
            wide_ref[h, pl.ds(start, slots)] = in_ref[at, h * lanes:(h + 1) * lanes].astype(F32)
        return jnp.minimum(start + counts_ref[s], cells)

    lax.fori_loop(0, shards, one, jnp.int32(0), unroll=4)
    for h in range(strips):
        at = slice(h * lanes, (h + 1) * lanes)
        for k in range(2):
            rows = wide_ref[h, pl.ds(k * half, half)].astype(BF)
            out_ref[pl.ds(k * half, half), at] = rows
            turned_ref[pl.ds((1 - k) * half, half), at] = rows


def rotate_kernel(own, p1, p2a, p2b, p3, near_ref, far_ref, last_ref, out_ref):
    cells, width = own.shape
    half = cells // 2
    tile = cells // 4
    for k in range(4):
        at = pl.ds(k * tile, tile)
        p2 = p2a[at] if k * tile < half else p2b[pl.ds(k * tile - half, tile)]
        other = p3[pl.ds((k * tile + half) % cells, tile)]
        near = (dot(own[at], near_ref[:width]) + dot(p1[at], near_ref[width:])).astype(BF)
        far = (dot(other, far_ref[:width]) + dot(p2, far_ref[width:])).astype(BF)
        out_ref[:, at] = (dot_nt(last_ref[:, :width], near) + dot_nt(last_ref[:, width:], far)).astype(BF)


def local_call(kernel, shapes, specs, scratch, name):
    outs = [jax.ShapeDtypeStruct(shape, BF) for shape in shapes]
    return pl.pallas_call(
        kernel,
        out_shape=outs,
        in_specs=[pl.BlockSpec(memory_space=m) for m in specs],
        out_specs=[pl.BlockSpec(memory_space=pltpu.VMEM) for _ in outs],
        scratch_shapes=scratch,
        compiler_params=pltpu.CompilerParams(vmem_limit_bytes=40 * 2**20),
        name=name,
    )


def body(snapshots, run_counts, route_counts):
    cells, width = snapshots.shape
    shards = lax.axis_size("space")
    runs = lax.axis_size("run")
    slots = 3 * cells // (2 * shards)
    run = lax.axis_index("run")
    spot = lax.axis_index("space")
    core = lax.rem(spot, 2)
    groups = [[2 * i + c for i in range(shards // 2)] for c in range(2)]

    def across(x, mask):
        return lax.ppermute(x, "run", [(r, r ^ mask) for r in range(runs)])

    def other_core(x):
        return lax.ppermute(x, "space", [(s, s ^ 1) for s in range(shards)])

    send = lax.dynamic_index_in_dim(route_counts, spot, 0, keepdims=False)
    recv = lax.dynamic_index_in_dim(route_counts, spot, 1, keepdims=False)
    smem, vmem = pltpu.SMEM, pltpu.VMEM
    wide = [pltpu.VMEM((width // 128, cells + 64, 128), F32)]
    keep = jnp.arange(width, dtype=jnp.int32) < run_counts[0]
    own = jnp.where(keep[None, :], snapshots, jnp.zeros((), BF))
    p1, p3 = across(own, 1), across(own, 3)
    [packed] = local_call(
        functools.partial(pack_kernel, shards, slots), [(shards * slots, width)], [smem, vmem], wide, "pack"
    )(send, own)
    arrived = lax.all_to_all(packed.reshape(shards, slots, width), "space", 0, 0, tiled=True)

    left = jnp.where(run < 2, own, p1)
    blocks = [dot_t(own, own), dot_t(own, p1), dot_t(left, p3)]
    half = width // 2

    def side(first):
        return jnp.concatenate([jnp.where(first, b[:, :half], b[:, half:]) for b in blocks], axis=1)

    mine = side(core == 0) + other_core(side(core == 1))
    mine, arrived = lax.optimization_barrier((mine, arrived))
    cut = mine.shape[1]
    routed, turned = local_call(
        functools.partial(unpack_kernel, shards, slots), [(cells, width)] * 2, [smem, vmem], wide, "unpack"
    )(recv, arrived.reshape(shards * slots, width))
    pieces = mine.reshape(shards // 2, -1, cut)
    pieces = lax.all_to_all(pieces, "space", 0, 0, tiled=True, axis_index_groups=groups)
    r1, r3 = across(routed, 1), across(turned, 3)
    pieces, routed = lax.optimization_barrier((pieces, routed))
    total = jnp.sum(pieces, axis=0)
    pieces = lax.all_to_all(
        jnp.broadcast_to(total, pieces.shape), "space", 0, 0, tiled=True, axis_index_groups=groups
    )
    spread = pieces.reshape(width, cut)
    on1, on3 = r1[:cells // 2], r3[:cells // 2]
    spread, r1, r3, on1, on3 = lax.optimization_barrier((spread, r1, r3, on1, on3))
    swap = other_core(spread)
    g3 = across(spread[:, :width], 3)
    g1 = across(spread[:, :half], 1)
    g2 = across(spread[:, :half], 2)
    c0 = jnp.where(
        core == 0,
        jnp.concatenate([spread[:, width:], swap[:, width:]], axis=1),
        jnp.concatenate([swap[:, width:], spread[:, width:]], axis=1),
    )
    g1, g2, g3, c0, swap, on1, on3 = lax.optimization_barrier((g1, g2, g3, c0, swap, on1, on3))
    r2a, r2b = across(on1, 3), across(on3, 1)
    mine = jnp.concatenate([g1, g2, g3], axis=1)
    crosses = [c0, across(c0, 1), across(c0, 2), across(c0, 3)]
    place = jnp.stack([run, core]).astype(jnp.int32)
    near, far, outer = level0(place, [spread, swap, mine, other_core(mine)], width)
    last = level1(place, near, far, outer, crosses, width, width // runs)
    [modes] = local_call(rotate_kernel, [(width // runs, cells)], [vmem] * 8, [], "rotate")(
        routed, r1, r2a, r2b, r3, near, far, last
    )
    return modes.T


def solution(mesh):
    in_specs = (P("space", "run"), P("run"), P())
    out_specs = P("space", "run")
    return jax.shard_map(body, mesh=mesh, in_specs=in_specs, out_specs=out_specs, check_vma=False)
```

```python
import functools
import math

import jax
import jax.numpy as jnp
from jax import lax
from jax.experimental import pallas as pl
from jax.experimental.pallas import tpu as pltpu
from jax.sharding import PartitionSpec as P

ITERS = 2
NS_STEPS = 8
BF = jnp.bfloat16
F32 = jnp.float32


def dot(a, b):
    return lax.dot_general(a, b, (((1,), (0,)), ((), ())), preferred_element_type=F32)


def dot_t(a, b):
    return lax.dot_general(a, b, (((0,), (0,)), ((), ())), preferred_element_type=F32)


def dot_nt(a, b):
    return lax.dot_general(a, b, (((1,), (1,)), ((), ())), preferred_element_type=F32)


def split(x):
    hi = x.astype(BF)
    return hi, (x - hi.astype(F32)).astype(BF)


def mul(a, b, op=dot):
    return op(a[0], b[0]) + (op(a[0], b[1]) + op(a[1], b[0]))


def half_mul(a, b, op=dot):
    return op(a[0], b) + op(a[1], b)


def half_mul_t(b, a):
    return dot_t(b, a[0]) + dot_t(b, a[1])


def solve(grams, eye):
    root = 1.0 / math.sqrt(2.0)
    gs = [(split(a), split(b), split(c)) for a, b, c in grams]
    heads = [((a + b) * root, (b.T + c) * root) for a, b, c in grams]
    for sweep in range(ITERS):
        scaled = []
        for pt, pb in heads:
            norm = lax.rsqrt(jnp.sum(pt * pt + pb * pb, keepdims=True) + 1e-06)
            scaled.append((split(pt * norm), split(pb * norm)))
        moments = [mul(st, st, dot_t) + mul(sb, sb, dot_t) for st, sb in scaled]
        turns = None
        ahead, fill = [], []
        for (a, b, c), (st, sb) in zip(gs, scaled):
            cell = [None] * 4
            ahead.append(cell)
            for n, f in enumerate((lambda a=a, st=st: mul(a, st), lambda b=b, sb=sb: mul(b, sb),
                                   lambda b=b, st=st: mul(b, st, dot_t), lambda c=c, sb=sb: mul(c, sb))):
                fill.append((cell, n, f))
        if sweep + 1 == ITERS:
            fill = []
        for k in range(NS_STEPS):
            last = k == NS_STEPS - 1
            halves = [split(m) for m in moments]
            weights = [1.5 * eye - 0.5 * m for m in moments]
            if not last:
                squares = [mul(h, h) for h in halves]
            turns = weights if k == 0 else [mul(split(t), split(w)) for t, w in zip(turns, weights)]
            for cell, n, f in fill[:len(grams)]:
                cell[n] = f()
            fill = fill[len(grams):]
            if not last:
                moments = [mul(h, split(2.25 * eye - 1.5 * m + 0.25 * q)) for h, m, q in zip(halves, moments, squares)]
        turns = [split(t) for t in turns]
        if sweep + 1 < ITERS:
            scaled = [(split(c[0] + c[1]), split(c[2] + c[3])) for c in ahead]
        heads = [(mul(st, t), mul(sb, t)) for (st, sb), t in zip(scaled, turns)]
    return heads


def identity(width):
    rows = lax.broadcasted_iota(jnp.int32, (width, width), 0)
    return (rows == lax.broadcasted_iota(jnp.int32, (width, width), 1)).astype(F32)


def level0_kernel(place_ref, *refs):
    parts, (near_ref, far_ref, outer_ref, own_ref, rest_ref, sems) = refs[:4], refs[4:]
    core = place_ref[1]
    copies = []
    for j, ref in enumerate((own_ref, rest_ref)):
        for k, slot in enumerate((core, 1 - core)):
            copies.append(pltpu.make_async_copy(parts[2 * j + k], ref.at[slot], sems.at[2 * j + k]))
    for c in copies:
        c.start()
    for c in copies:
        c.wait()
    width = near_ref.shape[1]
    half = width // 2

    def block(ref, n):
        at = slice(n * half, (n + 1) * half)
        return jnp.concatenate([ref[0, :, at], ref[1, :, at]], axis=1)

    near = (block(own_ref, 0), block(own_ref, 1), block(rest_ref, 0))
    far = (block(rest_ref, 2), block(rest_ref, 3), block(rest_ref, 1))
    grams = [near, far]
    bases = [(t.astype(BF), b.astype(BF)) for t, b in solve(grams, identity(width))]
    for i, ref in enumerate((near_ref, far_ref)):
        t, b = bases[i]
        ref[:width] = t
        ref[width:] = b
        g = [split(x) for x in grams[i]]
        up = half_mul(g[0], t) + half_mul(g[1], b)
        down = half_mul(g[1], t, dot_t) + half_mul(g[2], b)
        outer_ref[i] = half_mul_t(t, split(up)) + half_mul_t(b, split(down))


def level0(place, parts, width):
    half = width // 2
    return pl.pallas_call(
        level0_kernel,
        out_shape=[
            jax.ShapeDtypeStruct((2 * width, width), BF),
            jax.ShapeDtypeStruct((2 * width, width), BF),
            jax.ShapeDtypeStruct((2, width, width), F32),
        ],
        in_specs=[pl.BlockSpec(memory_space=pltpu.SMEM)] + [pl.BlockSpec(memory_space=pl.ANY)] * 4,
        scratch_shapes=[
            pltpu.VMEM((2, width, 3 * half), F32),
            pltpu.VMEM((2, width, 4 * half), F32),
            pltpu.SemaphoreType.DMA((4,)),
        ],
        compiler_params=pltpu.CompilerParams(vmem_limit_bytes=40 * 2**20),
        cost_estimate=pl.CostEstimate(flops=12 * 10**9, bytes_accessed=2 * 2**20, transcendentals=0),
        name="level0",
    )(place, *parts)


def level1_kernel(place_ref, near_ref, far_ref, outer_ref, c0_ref, c1_ref, c2_ref, c3_ref, last_ref, between_ref):
    run = place_ref[0]
    width = near_ref.shape[1]
    near = (near_ref[:width], near_ref[width:])
    far = (far_ref[width:], far_ref[:width])

    def between(first, second, f0, f1, s0, s1):
        (ft, fb), (st, sb) = first, second
        to_s1, to_s0, from_s0, from_s1 = (split(x[...]) for x in (f0, f1, s0, s1))
        up = half_mul(to_s1, sb) + half_mul(from_s1, st, dot_t)
        down = half_mul(to_s0, st) + half_mul(from_s0, sb, dot_t)
        return half_mul_t(ft, split(up)) + half_mul_t(fb, split(down))

    @pl.when(run < 2)
    def _():
        between_ref[...] = between(near, far, c0_ref, c1_ref, c2_ref, c3_ref)

    @pl.when(run >= 2)
    def _():
        between_ref[...] = between(far, near, c2_ref, c3_ref, c0_ref, c1_ref).T

    [(t, b)] = solve([(outer_ref[0], between_ref[...], outer_ref[1])], identity(width))
    quarter = last_ref.shape[0]
    pick_row = lax.broadcasted_iota(jnp.int32, (quarter, width), 0)
    pick_col = lax.broadcasted_iota(jnp.int32, (quarter, width), 1)
    pick = (pick_col == pick_row + run * quarter).astype(F32).astype(BF)
    last_ref[:, :width] = dot_nt(pick, t.astype(BF)).astype(BF)
    last_ref[:, width:] = dot_nt(pick, b.astype(BF)).astype(BF)


def level1(place, near, far, outer, crosses, width, quarter):
    return pl.pallas_call(
        level1_kernel,
        out_shape=jax.ShapeDtypeStruct((quarter, 2 * width), BF),
        in_specs=[pl.BlockSpec(memory_space=pltpu.SMEM)] + [pl.BlockSpec(memory_space=pltpu.VMEM)] * 7,
        out_specs=pl.BlockSpec(memory_space=pltpu.VMEM),
        scratch_shapes=[pltpu.VMEM((width, width), F32)],
        compiler_params=pltpu.CompilerParams(vmem_limit_bytes=40 * 2**20),
        cost_estimate=pl.CostEstimate(flops=8 * 10**9, bytes_accessed=2 * 2**20, transcendentals=0),
        name="level1",
    )(place, near, far, outer, *crosses)


def pack_kernel(shards, slots, counts_ref, rows_ref, out_ref, wide_ref):
    cells = rows_ref.shape[0]
    strips, _, lanes = wide_ref.shape
    pad = wide_ref.shape[1] - cells
    for h in range(strips):
        at = slice(h * lanes, (h + 1) * lanes)
        wide_ref[h, pl.ds(0, cells)] = rows_ref[:, at].astype(F32)
        wide_ref[h, pl.ds(cells, pad)] = jnp.zeros((pad, lanes), F32)

    def one(d, start):
        at = pl.ds(pl.multiple_of(d * slots, 16), slots)
        for h in range(strips):
            out_ref[at, h * lanes:(h + 1) * lanes] = wide_ref[h, pl.ds(start, slots)].astype(BF)
        return jnp.minimum(start + counts_ref[d], cells)

    lax.fori_loop(0, shards, one, jnp.int32(0), unroll=4)


def unpack_kernel(shards, slots, counts_ref, in_ref, out_ref, turned_ref, wide_ref):
    cells = out_ref.shape[0]
    half = cells // 2
    strips, _, lanes = wide_ref.shape

    def one(s, start):
        at = pl.ds(pl.multiple_of(s * slots, 16), slots)
        for h in range(strips):
            wide_ref[h, pl.ds(start, slots)] = in_ref[at, h * lanes:(h + 1) * lanes].astype(F32)
        return jnp.minimum(start + counts_ref[s], cells)

    lax.fori_loop(0, shards, one, jnp.int32(0), unroll=4)
    for h in range(strips):
        at = slice(h * lanes, (h + 1) * lanes)
        for k in range(2):
            rows = wide_ref[h, pl.ds(k * half, half)].astype(BF)
            out_ref[pl.ds(k * half, half), at] = rows
            turned_ref[pl.ds((1 - k) * half, half), at] = rows


def rotate_kernel(tiles, own, p1, p2a, p2b, p3, near_ref, far_ref, last_ref, out_ref):
    width = near_ref.shape[1]

    def turn(p2):
        near = (dot(own[...], near_ref[:width]) + dot(p1[...], near_ref[width:])).astype(BF)
        far = (dot(p3[...], far_ref[:width]) + dot(p2[...], far_ref[width:])).astype(BF)
        out_ref[...] = (dot_nt(last_ref[:, :width], near) + dot_nt(last_ref[:, width:], far)).astype(BF)

    @pl.when(pl.program_id(0) < tiles)
    def _():
        turn(p2a)

    @pl.when(pl.program_id(0) >= tiles)
    def _():
        turn(p2b)


def rotate(own, p1, p2a, p2b, p3, near, far, last):
    quarter = last.shape[0]
    tiles = 2
    cells, width = own.shape
    tile = cells // (2 * tiles)
    straight = pl.BlockSpec((tile, width), lambda i: (i, 0))
    low = pl.BlockSpec((tile, width), lambda i: (jnp.minimum(i, tiles - 1), 0))
    high = pl.BlockSpec((tile, width), lambda i: (jnp.maximum(i - tiles, 0), 0))
    swapped = pl.BlockSpec((tile, width), lambda i: (jnp.where(i < tiles, i + tiles, i - tiles), 0))
    whole = [pl.BlockSpec(x.shape, lambda i: (0, 0)) for x in (near, far, last)]
    return pl.pallas_call(
        functools.partial(rotate_kernel, tiles),
        grid=(2 * tiles,),
        out_shape=jax.ShapeDtypeStruct((quarter, cells), BF),
        in_specs=[straight, straight, low, high, swapped] + whole,
        out_specs=pl.BlockSpec((quarter, tile), lambda i: (0, i)),
        compiler_params=pltpu.CompilerParams(vmem_limit_bytes=40 * 2**20),
        name="rotate",
    )(own, p1, p2a, p2b, p3, near, far, last)


def local_call(kernel, shapes, specs, scratch, name):
    outs = [jax.ShapeDtypeStruct(shape, BF) for shape in shapes]
    return pl.pallas_call(
        kernel,
        out_shape=outs,
        in_specs=[pl.BlockSpec(memory_space=m) for m in specs],
        out_specs=[pl.BlockSpec(memory_space=pltpu.VMEM) for _ in outs],
        scratch_shapes=scratch,
        compiler_params=pltpu.CompilerParams(vmem_limit_bytes=40 * 2**20),
        name=name,
    )


def body(snapshots, run_counts, route_counts):
    cells, width = snapshots.shape
    shards = lax.axis_size("space")
    runs = lax.axis_size("run")
    slots = 3 * cells // (2 * shards)
    run = lax.axis_index("run")
    spot = lax.axis_index("space")
    core = lax.rem(spot, 2)
    groups = [[2 * i + c for i in range(shards // 2)] for c in range(2)]

    def across(x, mask):
        return lax.ppermute(x, "run", [(r, r ^ mask) for r in range(runs)])

    def other_core(x):
        return lax.ppermute(x, "space", [(s, s ^ 1) for s in range(shards)])

    send = lax.dynamic_index_in_dim(route_counts, spot, 0, keepdims=False)
    recv = lax.dynamic_index_in_dim(route_counts, spot, 1, keepdims=False)
    smem, vmem = pltpu.SMEM, pltpu.VMEM
    wide = [pltpu.VMEM((width // 128, cells + 64, 128), F32)]
    keep = jnp.arange(width, dtype=jnp.int32) < run_counts[0]
    own = jnp.where(keep[None, :], snapshots, jnp.zeros((), BF))
    p1, p3 = across(own, 1), across(own, 3)
    [packed] = local_call(
        functools.partial(pack_kernel, shards, slots), [(shards * slots, width)], [smem, vmem], wide, "pack"
    )(send, own)
    arrived = lax.all_to_all(packed.reshape(shards, slots, width), "space", 0, 0, tiled=True)

    left = jnp.where(run < 2, own, p1)
    blocks = [dot_t(own, own), dot_t(own, p1), dot_t(left, p3)]
    half = width // 2

    def side(first):
        return jnp.concatenate([jnp.where(first, b[:, :half], b[:, half:]) for b in blocks], axis=1)

    mine = side(core == 0) + other_core(side(core == 1))
    mine, arrived = lax.optimization_barrier((mine, arrived))
    cut = mine.shape[1]
    routed, turned = local_call(
        functools.partial(unpack_kernel, shards, slots), [(cells, width)] * 2, [smem, vmem], wide, "unpack"
    )(recv, arrived.reshape(shards * slots, width))
    pieces = mine.reshape(shards // 2, -1, cut)
    pieces = lax.all_to_all(pieces, "space", 0, 0, tiled=True, axis_index_groups=groups)
    r1, r3 = across(routed, 1), across(turned, 3)
    pieces, routed = lax.optimization_barrier((pieces, routed))
    total = jnp.sum(pieces, axis=0)
    pieces = lax.all_to_all(
        jnp.broadcast_to(total, pieces.shape), "space", 0, 0, tiled=True, axis_index_groups=groups
    )
    spread = pieces.reshape(width, cut)
    on1, on3 = r1[:cells // 2], r3[:cells // 2]
    spread, r1, r3, on1, on3 = lax.optimization_barrier((spread, r1, r3, on1, on3))
    swap = other_core(spread)
    g3 = across(spread[:, :width], 3)
    g1 = across(spread[:, :half], 1)
    g2 = across(spread[:, :half], 2)
    c0 = jnp.where(
        core == 0,
        jnp.concatenate([spread[:, width:], swap[:, width:]], axis=1),
        jnp.concatenate([swap[:, width:], spread[:, width:]], axis=1),
    )
    g1, g2, g3, c0, swap = lax.optimization_barrier((g1, g2, g3, c0, swap))
    mine = jnp.concatenate([g1, g2, g3], axis=1)
    crosses = [c0, across(c0, 1), across(c0, 2), across(c0, 3)]
    place = jnp.stack([run, core]).astype(jnp.int32)
    near, far, outer = level0(place, [spread, swap, mine, other_core(mine)], width)
    near, on1, on3 = lax.optimization_barrier((near, on1, on3))
    r2a, r2b = across(on1, 3), across(on3, 1)
    last = level1(place, near, far, outer, crosses, width, width // runs)
    return rotate(routed, r1, r2a, r2b, r3, near, far, last).T


def solution(mesh):
    in_specs = (P("space", "run"), P("run"), P())
    out_specs = P("space", "run")
    return jax.shard_map(body, mesh=mesh, in_specs=in_specs, out_specs=out_specs, check_vma=False)
```

```python
import functools
import math

import jax
import jax.numpy as jnp
from jax import lax
from jax.experimental import pallas as pl
from jax.experimental.pallas import tpu as pltpu
from jax.sharding import PartitionSpec as P

ITERS = 2
NS_STEPS = 8
BF = jnp.bfloat16
F32 = jnp.float32


def dot(a, b):
    return lax.dot_general(a, b, (((1,), (0,)), ((), ())), preferred_element_type=F32)


def dot_t(a, b):
    return lax.dot_general(a, b, (((0,), (0,)), ((), ())), preferred_element_type=F32)


def dot_nt(a, b):
    return lax.dot_general(a, b, (((1,), (1,)), ((), ())), preferred_element_type=F32)


def split(x):
    hi = x.astype(BF)
    return hi, (x - hi.astype(F32)).astype(BF)


def mul(a, b, op=dot):
    return op(a[0], b[0]) + (op(a[0], b[1]) + op(a[1], b[0]))


def half_mul(a, b, op=dot):
    return op(a[0], b) + op(a[1], b)


def half_mul_t(b, a):
    return dot_t(b, a[0]) + dot_t(b, a[1])


def solve(grams, eye):
    root = 1.0 / math.sqrt(2.0)
    gs = [(split(a), split(b), split(c)) for a, b, c in grams]
    heads = [((a + b) * root, (b.T + c) * root) for a, b, c in grams]
    for sweep in range(ITERS):
        scaled = []
        for pt, pb in heads:
            norm = lax.rsqrt(jnp.sum(pt * pt + pb * pb, keepdims=True) + 1e-06)
            scaled.append((split(pt * norm), split(pb * norm)))
        moments = [mul(st, st, dot_t) + mul(sb, sb, dot_t) for st, sb in scaled]
        turns = None
        ahead, fill = [], []
        for (a, b, c), (st, sb) in zip(gs, scaled):
            cell = [None] * 4
            ahead.append(cell)
            for n, f in enumerate((lambda a=a, st=st: mul(a, st), lambda b=b, sb=sb: mul(b, sb),
                                   lambda b=b, st=st: mul(b, st, dot_t), lambda c=c, sb=sb: mul(c, sb))):
                fill.append((cell, n, f))
        if sweep + 1 == ITERS:
            fill = []
        for k in range(NS_STEPS):
            last = k == NS_STEPS - 1
            halves = [split(m) for m in moments]
            weights = [1.5 * eye - 0.5 * m for m in moments]
            if not last:
                squares = [mul(h, h) for h in halves]
            turns = weights if k == 0 else [mul(split(t), split(w)) for t, w in zip(turns, weights)]
            for cell, n, f in fill[:len(grams)]:
                cell[n] = f()
            fill = fill[len(grams):]
            if not last:
                moments = [mul(h, split(2.25 * eye - 1.5 * m + 0.25 * q)) for h, m, q in zip(halves, moments, squares)]
        turns = [split(t) for t in turns]
        if sweep + 1 < ITERS:
            scaled = [(split(c[0] + c[1]), split(c[2] + c[3])) for c in ahead]
        heads = [(mul(st, t), mul(sb, t)) for (st, sb), t in zip(scaled, turns)]
    return heads


def identity(width):
    rows = lax.broadcasted_iota(jnp.int32, (width, width), 0)
    return (rows == lax.broadcasted_iota(jnp.int32, (width, width), 1)).astype(F32)


def level0_kernel(place_ref, *refs):
    parts, (near_ref, far_ref, outer_ref, own_ref, rest_ref, sems) = refs[:4], refs[4:]
    core = place_ref[1]
    copies = []
    for j, ref in enumerate((own_ref, rest_ref)):
        for k, slot in enumerate((core, 1 - core)):
            copies.append(pltpu.make_async_copy(parts[2 * j + k], ref.at[slot], sems.at[2 * j + k]))
    for c in copies:
        c.start()
    for c in copies:
        c.wait()
    width = near_ref.shape[1]
    half = width // 2

    def block(ref, n):
        at = slice(n * half, (n + 1) * half)
        return jnp.concatenate([ref[0, :, at], ref[1, :, at]], axis=1)

    near = (block(own_ref, 0), block(own_ref, 1), block(rest_ref, 0))
    far = (block(rest_ref, 2), block(rest_ref, 3), block(rest_ref, 1))
    grams = [near, far]
    bases = [(t.astype(BF), b.astype(BF)) for t, b in solve(grams, identity(width))]
    for i, ref in enumerate((near_ref, far_ref)):
        t, b = bases[i]
        ref[:width] = t
        ref[width:] = b
        g = [split(x) for x in grams[i]]
        up = half_mul(g[0], t) + half_mul(g[1], b)
        down = half_mul(g[1], t, dot_t) + half_mul(g[2], b)
        outer_ref[i] = half_mul_t(t, split(up)) + half_mul_t(b, split(down))


def level0(place, parts, width):
    half = width // 2
    return pl.pallas_call(
        level0_kernel,
        out_shape=[
            jax.ShapeDtypeStruct((2 * width, width), BF),
            jax.ShapeDtypeStruct((2 * width, width), BF),
            jax.ShapeDtypeStruct((2, width, width), F32),
        ],
        in_specs=[pl.BlockSpec(memory_space=pltpu.SMEM)] + [pl.BlockSpec(memory_space=pl.ANY)] * 4,
        scratch_shapes=[
            pltpu.VMEM((2, width, 3 * half), F32),
            pltpu.VMEM((2, width, 4 * half), F32),
            pltpu.SemaphoreType.DMA((4,)),
        ],
        compiler_params=pltpu.CompilerParams(vmem_limit_bytes=40 * 2**20),
        cost_estimate=pl.CostEstimate(flops=12 * 10**9, bytes_accessed=2 * 2**20, transcendentals=0),
        name="level0",
    )(place, *parts)


def level1_kernel(place_ref, near_ref, far_ref, outer_ref, c0_ref, c1_ref, c2_ref, c3_ref, last_ref, between_ref):
    run = place_ref[0]
    width = near_ref.shape[1]
    near = (near_ref[:width], near_ref[width:])
    far = (far_ref[width:], far_ref[:width])

    def between(first, second, f0, f1, s0, s1):
        (ft, fb), (st, sb) = first, second
        to_s1, to_s0, from_s0, from_s1 = (split(x[...]) for x in (f0, f1, s0, s1))
        up = half_mul(to_s1, sb) + half_mul(from_s1, st, dot_t)
        down = half_mul(to_s0, st) + half_mul(from_s0, sb, dot_t)
        return half_mul_t(ft, split(up)) + half_mul_t(fb, split(down))

    @pl.when(run < 2)
    def _():
        between_ref[...] = between(near, far, c0_ref, c1_ref, c2_ref, c3_ref)

    @pl.when(run >= 2)
    def _():
        between_ref[...] = between(far, near, c2_ref, c3_ref, c0_ref, c1_ref).T

    [(t, b)] = solve([(outer_ref[0], between_ref[...], outer_ref[1])], identity(width))
    quarter = last_ref.shape[0]
    pick_row = lax.broadcasted_iota(jnp.int32, (quarter, width), 0)
    pick_col = lax.broadcasted_iota(jnp.int32, (quarter, width), 1)
    pick = (pick_col == pick_row + run * quarter).astype(F32).astype(BF)
    last_ref[:, :width] = dot_nt(pick, t.astype(BF)).astype(BF)
    last_ref[:, width:] = dot_nt(pick, b.astype(BF)).astype(BF)


def level1(place, near, far, outer, crosses, width, quarter):
    return pl.pallas_call(
        level1_kernel,
        out_shape=jax.ShapeDtypeStruct((quarter, 2 * width), BF),
        in_specs=[pl.BlockSpec(memory_space=pltpu.SMEM)] + [pl.BlockSpec(memory_space=pltpu.VMEM)] * 7,
        out_specs=pl.BlockSpec(memory_space=pltpu.VMEM),
        scratch_shapes=[pltpu.VMEM((width, width), F32)],
        compiler_params=pltpu.CompilerParams(vmem_limit_bytes=40 * 2**20),
        cost_estimate=pl.CostEstimate(flops=8 * 10**9, bytes_accessed=2 * 2**20, transcendentals=0),
        name="level1",
    )(place, near, far, outer, *crosses)


def pack_kernel(shards, slots, valid_ref, counts_ref, rows_ref, own_ref, out_ref, wide_ref, landed_ref, sems):
    cells = own_ref.shape[0]
    strips, _, lanes = wide_ref.shape
    pad = wide_ref.shape[1] - cells
    tile = cells // 4
    copies = []
    for k in range(4):
        at = pl.ds(k * tile, tile)
        copies.append(pltpu.make_async_copy(rows_ref.at[at], landed_ref.at[at], sems.at[k]))
        copies[-1].start()
    keep = [lax.broadcasted_iota(jnp.int32, (tile, lanes), 1) + h * lanes < valid_ref[0] for h in range(strips)]
    for h in range(strips):
        wide_ref[h, pl.ds(cells, pad)] = jnp.zeros((pad, lanes), F32)
    for k in range(4):
        at = pl.ds(k * tile, tile)
        copies[k].wait()
        for h in range(strips):
            lane = slice(h * lanes, (h + 1) * lanes)
            rows = jnp.where(keep[h], landed_ref[at, lane].astype(F32), 0.0)
            own_ref[at, lane] = rows.astype(BF)
            wide_ref[h, at] = rows

    def one(d, start):
        at = pl.ds(pl.multiple_of(d * slots, 16), slots)
        for h in range(strips):
            out_ref[at, h * lanes:(h + 1) * lanes] = wide_ref[h, pl.ds(start, slots)].astype(BF)
        return jnp.minimum(start + counts_ref[d], cells)

    lax.fori_loop(0, shards, one, jnp.int32(0), unroll=4)


def unpack_kernel(shards, slots, counts_ref, in_ref, out_ref, turned_ref, wide_ref):
    cells = out_ref.shape[0]
    half = cells // 2
    strips, _, lanes = wide_ref.shape

    def one(s, start):
        at = pl.ds(pl.multiple_of(s * slots, 16), slots)
        for h in range(strips):
            wide_ref[h, pl.ds(start, slots)] = in_ref[at, h * lanes:(h + 1) * lanes].astype(F32)
        return jnp.minimum(start + counts_ref[s], cells)

    lax.fori_loop(0, shards, one, jnp.int32(0), unroll=4)
    for h in range(strips):
        at = slice(h * lanes, (h + 1) * lanes)
        for k in range(2):
            rows = wide_ref[h, pl.ds(k * half, half)].astype(BF)
            out_ref[pl.ds(k * half, half), at] = rows
            turned_ref[pl.ds((1 - k) * half, half), at] = rows


def rotate_kernel(own, p1, p2a, p2b, p3, near_ref, far_ref, last_ref, out_ref, modes_ref, sems):
    cells, width = own.shape
    half = cells // 2
    tile = cells // 4
    copies = []
    for k in range(4):
        at = pl.ds(k * tile, tile)
        p2 = p2a[at] if k * tile < half else p2b[pl.ds(k * tile - half, tile)]
        other = p3[pl.ds((k * tile + half) % cells, tile)]
        near = (dot(own[at], near_ref[:width]) + dot(p1[at], near_ref[width:])).astype(BF)
        far = (dot(other, far_ref[:width]) + dot(p2, far_ref[width:])).astype(BF)
        modes_ref[:, at] = (dot_nt(last_ref[:, :width], near) + dot_nt(last_ref[:, width:], far)).astype(BF)
        copies.append(pltpu.make_async_copy(modes_ref.at[:, at], out_ref.at[:, at], sems.at[k]))
        copies[-1].start()
    for c in copies:
        c.wait()


def local_call(kernel, shapes, specs, scratch, name, out=pltpu.VMEM, room=40):
    outs = [jax.ShapeDtypeStruct(shape, BF) for shape in shapes]
    return pl.pallas_call(
        kernel,
        out_shape=outs,
        in_specs=[pl.BlockSpec(memory_space=m) for m in specs],
        out_specs=[pl.BlockSpec(memory_space=out) for _ in outs],
        scratch_shapes=scratch,
        compiler_params=pltpu.CompilerParams(vmem_limit_bytes=room * 2**20),
        name=name,
    )


def body(snapshots, run_counts, route_counts):
    cells, width = snapshots.shape
    shards = lax.axis_size("space")
    runs = lax.axis_size("run")
    slots = 3 * cells // (2 * shards)
    run = lax.axis_index("run")
    spot = lax.axis_index("space")
    core = lax.rem(spot, 2)
    groups = [[2 * i + c for i in range(shards // 2)] for c in range(2)]

    def across(x, mask):
        return lax.ppermute(x, "run", [(r, r ^ mask) for r in range(runs)])

    def other_core(x):
        return lax.ppermute(x, "space", [(s, s ^ 1) for s in range(shards)])

    send = lax.dynamic_index_in_dim(route_counts, spot, 0, keepdims=False)
    recv = lax.dynamic_index_in_dim(route_counts, spot, 1, keepdims=False)
    smem, vmem = pltpu.SMEM, pltpu.VMEM
    wide = [pltpu.VMEM((width // 128, cells + 64, 128), F32)]
    own, packed = local_call(
        functools.partial(pack_kernel, shards, slots), [(cells, width), (shards * slots, width)],
        [smem, smem, pltpu.HBM], wide + [pltpu.VMEM((cells, width), BF), pltpu.SemaphoreType.DMA((4,))], "mask_and_pack", room=60,
    )(run_counts, send, snapshots)
    p1, p3 = across(own, 1), across(own, 3)
    arrived = lax.all_to_all(packed.reshape(shards, slots, width), "space", 0, 0, tiled=True)

    left = jnp.where(run < 2, own, p1)
    blocks = [dot_t(own, own), dot_t(own, p1), dot_t(left, p3)]
    half = width // 2

    def side(first):
        return jnp.concatenate([jnp.where(first, b[:, :half], b[:, half:]) for b in blocks], axis=1)

    mine = side(core == 0) + other_core(side(core == 1))
    mine, arrived = lax.optimization_barrier((mine, arrived))
    cut = mine.shape[1]
    routed, turned = local_call(
        functools.partial(unpack_kernel, shards, slots), [(cells, width)] * 2, [smem, vmem], wide, "unpack"
    )(recv, arrived.reshape(shards * slots, width))
    pieces = mine.reshape(shards // 2, -1, cut)
    pieces = lax.all_to_all(pieces, "space", 0, 0, tiled=True, axis_index_groups=groups)
    r1, r3 = across(routed, 1), across(turned, 3)
    pieces, routed = lax.optimization_barrier((pieces, routed))
    total = jnp.sum(pieces, axis=0)
    pieces = lax.all_to_all(
        jnp.broadcast_to(total, pieces.shape), "space", 0, 0, tiled=True, axis_index_groups=groups
    )
    spread = pieces.reshape(width, cut)
    on1, on3 = r1[:cells // 2], r3[:cells // 2]
    spread, r1, r3, on1, on3 = lax.optimization_barrier((spread, r1, r3, on1, on3))
    swap = other_core(spread)
    g3 = across(spread[:, :width], 3)
    g1 = across(spread[:, :half], 1)
    g2 = across(spread[:, :half], 2)
    c0 = jnp.where(
        core == 0,
        jnp.concatenate([spread[:, width:], swap[:, width:]], axis=1),
        jnp.concatenate([swap[:, width:], spread[:, width:]], axis=1),
    )
    g1, g2, g3, c0, swap = lax.optimization_barrier((g1, g2, g3, c0, swap))
    mine = jnp.concatenate([g1, g2, g3], axis=1)
    crosses = [c0, across(c0, 1), across(c0, 2), across(c0, 3)]
    place = jnp.stack([run, core]).astype(jnp.int32)
    near, far, outer = level0(place, [spread, swap, mine, other_core(mine)], width)
    near, on1, on3 = lax.optimization_barrier((near, on1, on3))
    r2a, r2b = across(on1, 3), across(on3, 1)
    last = level1(place, near, far, outer, crosses, width, width // runs)
    shape = (width // runs, cells)
    room = [pltpu.VMEM(shape, BF), pltpu.SemaphoreType.DMA((4,))]
    [modes] = local_call(rotate_kernel, [shape], [vmem] * 8, room, "rotate", pltpu.HBM)(
        routed, r1, r2a, r2b, r3, near, far, last
    )
    return modes.T


def solution(mesh):
    in_specs = (P("space", "run"), P("run"), P())
    out_specs = P("space", "run")
    return jax.shard_map(body, mesh=mesh, in_specs=in_specs, out_specs=out_specs, check_vma=False)
```

```python
import functools
import math

import jax
import jax.numpy as jnp
from jax import lax
from jax.experimental import pallas as pl
from jax.experimental.pallas import tpu as pltpu
from jax.sharding import PartitionSpec as P

ITERS = 2
NS_STEPS = 8
BF = jnp.bfloat16
F32 = jnp.float32


def dot(a, b):
    return lax.dot_general(a, b, (((1,), (0,)), ((), ())), preferred_element_type=F32)


def dot_t(a, b):
    return lax.dot_general(a, b, (((0,), (0,)), ((), ())), preferred_element_type=F32)


def dot_nt(a, b):
    return lax.dot_general(a, b, (((1,), (1,)), ((), ())), preferred_element_type=F32)


def split(x):
    hi = x.astype(BF)
    return hi, (x - hi.astype(F32)).astype(BF)


def mul(a, b, op=dot):
    return op(a[0], b[0]) + (op(a[0], b[1]) + op(a[1], b[0]))


def half_mul(a, b, op=dot):
    return op(a[0], b) + op(a[1], b)


def half_mul_t(b, a):
    return dot_t(b, a[0]) + dot_t(b, a[1])


def solve(grams, eye):
    root = 1.0 / math.sqrt(2.0)
    gs = [(split(a), split(b), split(c)) for a, b, c in grams]
    heads = [((a + b) * root, (b.T + c) * root) for a, b, c in grams]
    for sweep in range(ITERS):
        scaled = []
        for pt, pb in heads:
            norm = lax.rsqrt(jnp.sum(pt * pt + pb * pb, keepdims=True) + 1e-06)
            scaled.append((split(pt * norm), split(pb * norm)))
        moments = [mul(st, st, dot_t) + mul(sb, sb, dot_t) for st, sb in scaled]
        turns = None
        ahead, fill = [], []
        for (a, b, c), (st, sb) in zip(gs, scaled):
            cell = [None] * 4
            ahead.append(cell)
            for n, f in enumerate((lambda a=a, st=st: mul(a, st), lambda b=b, sb=sb: mul(b, sb),
                                   lambda b=b, st=st: mul(b, st, dot_t), lambda c=c, sb=sb: mul(c, sb))):
                fill.append((cell, n, f))
        if sweep + 1 == ITERS:
            fill = []
        for k in range(NS_STEPS):
            last = k == NS_STEPS - 1
            halves = [split(m) for m in moments]
            weights = [1.5 * eye - 0.5 * m for m in moments]
            if not last:
                squares = [mul(h, h) for h in halves]
            turns = weights if k == 0 else [mul(split(t), split(w)) for t, w in zip(turns, weights)]
            for cell, n, f in fill[:len(grams)]:
                cell[n] = f()
            fill = fill[len(grams):]
            if not last:
                moments = [mul(h, split(2.25 * eye - 1.5 * m + 0.25 * q)) for h, m, q in zip(halves, moments, squares)]
        turns = [split(t) for t in turns]
        if sweep + 1 < ITERS:
            scaled = [(split(c[0] + c[1]), split(c[2] + c[3])) for c in ahead]
        heads = [(mul(st, t), mul(sb, t)) for (st, sb), t in zip(scaled, turns)]
    return heads


def identity(width):
    rows = lax.broadcasted_iota(jnp.int32, (width, width), 0)
    return (rows == lax.broadcasted_iota(jnp.int32, (width, width), 1)).astype(F32)


def level0_kernel(place_ref, *refs):
    parts, (near_ref, far_ref, outer_ref, own_ref, rest_ref, sems) = refs[:4], refs[4:]
    core = place_ref[1]
    copies = []
    for j, ref in enumerate((own_ref, rest_ref)):
        for k, slot in enumerate((core, 1 - core)):
            copies.append(pltpu.make_async_copy(parts[2 * j + k], ref.at[slot], sems.at[2 * j + k]))
    for c in copies:
        c.start()
    for c in copies:
        c.wait()
    width = near_ref.shape[1]
    half = width // 2

    def block(ref, n):
        at = slice(n * half, (n + 1) * half)
        return jnp.concatenate([ref[0, :, at], ref[1, :, at]], axis=1)

    near = (block(own_ref, 0), block(own_ref, 1), block(rest_ref, 0))
    far = (block(rest_ref, 2), block(rest_ref, 3), block(rest_ref, 1))
    grams = [near, far]
    bases = [(t.astype(BF), b.astype(BF)) for t, b in solve(grams, identity(width))]
    for i, ref in enumerate((near_ref, far_ref)):
        t, b = bases[i]
        ref[:width] = t
        ref[width:] = b
        g = [split(x) for x in grams[i]]
        up = half_mul(g[0], t) + half_mul(g[1], b)
        down = half_mul(g[1], t, dot_t) + half_mul(g[2], b)
        outer_ref[i] = half_mul_t(t, split(up)) + half_mul_t(b, split(down))


def level0(place, parts, width):
    half = width // 2
    return pl.pallas_call(
        level0_kernel,
        out_shape=[
            jax.ShapeDtypeStruct((2 * width, width), BF),
            jax.ShapeDtypeStruct((2 * width, width), BF),
            jax.ShapeDtypeStruct((2, width, width), F32),
        ],
        in_specs=[pl.BlockSpec(memory_space=pltpu.SMEM)] + [pl.BlockSpec(memory_space=pl.ANY)] * 4,
        scratch_shapes=[
            pltpu.VMEM((2, width, 3 * half), F32),
            pltpu.VMEM((2, width, 4 * half), F32),
            pltpu.SemaphoreType.DMA((4,)),
        ],
        compiler_params=pltpu.CompilerParams(vmem_limit_bytes=40 * 2**20),
        cost_estimate=pl.CostEstimate(flops=12 * 10**9, bytes_accessed=2 * 2**20, transcendentals=0),
        name="level0",
    )(place, *parts)


def level1_kernel(place_ref, near_ref, far_ref, outer_ref, c0_ref, c1_ref, c2_ref, c3_ref, last_ref, between_ref):
    run = place_ref[0]
    width = near_ref.shape[1]
    near = (near_ref[:width], near_ref[width:])
    far = (far_ref[width:], far_ref[:width])

    def between(first, second, f0, f1, s0, s1):
        (ft, fb), (st, sb) = first, second
        to_s1, to_s0, from_s0, from_s1 = (split(x[...]) for x in (f0, f1, s0, s1))
        up = half_mul(to_s1, sb) + half_mul(from_s1, st, dot_t)
        down = half_mul(to_s0, st) + half_mul(from_s0, sb, dot_t)
        return half_mul_t(ft, split(up)) + half_mul_t(fb, split(down))

    @pl.when(run < 2)
    def _():
        between_ref[...] = between(near, far, c0_ref, c1_ref, c2_ref, c3_ref)

    @pl.when(run >= 2)
    def _():
        between_ref[...] = between(far, near, c2_ref, c3_ref, c0_ref, c1_ref).T

    [(t, b)] = solve([(outer_ref[0], between_ref[...], outer_ref[1])], identity(width))
    quarter = last_ref.shape[0]
    pick_row = lax.broadcasted_iota(jnp.int32, (quarter, width), 0)
    pick_col = lax.broadcasted_iota(jnp.int32, (quarter, width), 1)
    pick = (pick_col == pick_row + run * quarter).astype(F32).astype(BF)
    last_ref[:, :width] = dot_nt(pick, t.astype(BF)).astype(BF)
    last_ref[:, width:] = dot_nt(pick, b.astype(BF)).astype(BF)


def level1(place, near, far, outer, crosses, width, quarter):
    return pl.pallas_call(
        level1_kernel,
        out_shape=jax.ShapeDtypeStruct((quarter, 2 * width), BF),
        in_specs=[pl.BlockSpec(memory_space=pltpu.SMEM)] + [pl.BlockSpec(memory_space=pltpu.VMEM)] * 7,
        out_specs=pl.BlockSpec(memory_space=pltpu.VMEM),
        scratch_shapes=[pltpu.VMEM((width, width), F32)],
        compiler_params=pltpu.CompilerParams(vmem_limit_bytes=40 * 2**20),
        cost_estimate=pl.CostEstimate(flops=8 * 10**9, bytes_accessed=2 * 2**20, transcendentals=0),
        name="level1",
    )(place, near, far, outer, *crosses)


def pack_kernel(shards, slots, counts_ref, rows_ref, out_ref, wide_ref):
    cells = rows_ref.shape[0]
    strips, _, lanes = wide_ref.shape
    pad = wide_ref.shape[1] - cells
    for h in range(strips):
        at = slice(h * lanes, (h + 1) * lanes)
        wide_ref[h, pl.ds(0, cells)] = rows_ref[:, at].astype(F32)
        wide_ref[h, pl.ds(cells, pad)] = jnp.zeros((pad, lanes), F32)

    def one(d, start):
        at = pl.ds(pl.multiple_of(d * slots, 16), slots)
        for h in range(strips):
            out_ref[at, h * lanes:(h + 1) * lanes] = wide_ref[h, pl.ds(start, slots)].astype(BF)
        return jnp.minimum(start + counts_ref[d], cells)

    lax.fori_loop(0, shards, one, jnp.int32(0), unroll=4)


def unpack_kernel(shards, slots, counts_ref, in_ref, out_ref, turned_ref, wide_ref):
    cells = out_ref.shape[0]
    half = cells // 2
    strips, _, lanes = wide_ref.shape

    def one(s, start):
        at = pl.ds(pl.multiple_of(s * slots, 16), slots)
        for h in range(strips):
            wide_ref[h, pl.ds(start, slots)] = in_ref[at, h * lanes:(h + 1) * lanes].astype(F32)
        return jnp.minimum(start + counts_ref[s], cells)

    lax.fori_loop(0, shards, one, jnp.int32(0), unroll=4)
    for h in range(strips):
        at = slice(h * lanes, (h + 1) * lanes)
        for k in range(2):
            rows = wide_ref[h, pl.ds(k * half, half)].astype(BF)
            out_ref[pl.ds(k * half, half), at] = rows
            turned_ref[pl.ds((1 - k) * half, half), at] = rows


def rotate_kernel(own, p1, p2a, p2b, p3, near_ref, far_ref, last_ref, out_ref):
    step, steps = pl.program_id(0), pl.num_programs(0)
    cells, width = own.shape
    tile = out_ref.shape[1]
    half = cells // 2
    first = pl.multiple_of(step * tile, tile)

    def turn(p2, inside, other):
        at = pl.ds(first, tile)
        near = (dot(own[at], near_ref[:width]) + dot(p1[at], near_ref[width:])).astype(BF)
        rows = p2[pl.ds(pl.multiple_of(inside, tile), tile)]
        mate = p3[pl.ds(pl.multiple_of(other, tile), tile)]
        far = (dot(mate, far_ref[:width]) + dot(rows, far_ref[width:])).astype(BF)
        out_ref[...] = (dot_nt(last_ref[:, :width], near) + dot_nt(last_ref[:, width:], far)).astype(BF)

    @pl.when(step < steps // 2)
    def _():
        turn(p2a, first, first + half)

    @pl.when(step >= steps // 2)
    def _():
        turn(p2b, first - half, first - half)


def rotate(own, p1, p2a, p2b, p3, near, far, last):
    quarter, steps = last.shape[0], 4
    cells = own.shape[0]
    return pl.pallas_call(
        rotate_kernel,
        grid=(steps,),
        out_shape=jax.ShapeDtypeStruct((quarter, cells), BF),
        in_specs=[pl.BlockSpec(memory_space=pltpu.VMEM)] * 8,
        out_specs=pl.BlockSpec((quarter, cells // steps), lambda i: (0, i)),
        compiler_params=pltpu.CompilerParams(vmem_limit_bytes=40 * 2**20),
        name="rotate",
    )(own, p1, p2a, p2b, p3, near, far, last)


def local_call(kernel, shapes, specs, scratch, name):
    outs = [jax.ShapeDtypeStruct(shape, BF) for shape in shapes]
    return pl.pallas_call(
        kernel,
        out_shape=outs,
        in_specs=[pl.BlockSpec(memory_space=m) for m in specs],
        out_specs=[pl.BlockSpec(memory_space=pltpu.VMEM) for _ in outs],
        scratch_shapes=scratch,
        compiler_params=pltpu.CompilerParams(vmem_limit_bytes=40 * 2**20),
        name=name,
    )


def body(snapshots, run_counts, route_counts):
    cells, width = snapshots.shape
    shards = lax.axis_size("space")
    runs = lax.axis_size("run")
    slots = 3 * cells // (2 * shards)
    run = lax.axis_index("run")
    spot = lax.axis_index("space")
    core = lax.rem(spot, 2)
    groups = [[2 * i + c for i in range(shards // 2)] for c in range(2)]

    def across(x, mask):
        return lax.ppermute(x, "run", [(r, r ^ mask) for r in range(runs)])

    def other_core(x):
        return lax.ppermute(x, "space", [(s, s ^ 1) for s in range(shards)])

    send = lax.dynamic_index_in_dim(route_counts, spot, 0, keepdims=False)
    recv = lax.dynamic_index_in_dim(route_counts, spot, 1, keepdims=False)
    smem, vmem = pltpu.SMEM, pltpu.VMEM
    wide = [pltpu.VMEM((width // 128, cells + 64, 128), F32)]
    keep = jnp.arange(width, dtype=jnp.int32) < run_counts[0]
    own = jnp.where(keep[None, :], snapshots, jnp.zeros((), BF))
    p1, p3 = across(own, 1), across(own, 3)
    [packed] = local_call(
        functools.partial(pack_kernel, shards, slots), [(shards * slots, width)], [smem, vmem], wide, "pack"
    )(send, own)
    arrived = lax.all_to_all(packed.reshape(shards, slots, width), "space", 0, 0, tiled=True)

    left = jnp.where(run < 2, own, p1)
    blocks = [dot_t(own, own), dot_t(own, p1), dot_t(left, p3)]
    half = width // 2

    def side(first):
        return jnp.concatenate([jnp.where(first, b[:, :half], b[:, half:]) for b in blocks], axis=1)

    mine = side(core == 0) + other_core(side(core == 1))
    mine, arrived = lax.optimization_barrier((mine, arrived))
    cut = mine.shape[1]
    routed, turned = local_call(
        functools.partial(unpack_kernel, shards, slots), [(cells, width)] * 2, [smem, vmem], wide, "unpack"
    )(recv, arrived.reshape(shards * slots, width))
    pieces = mine.reshape(shards // 2, -1, cut)
    pieces = lax.all_to_all(pieces, "space", 0, 0, tiled=True, axis_index_groups=groups)
    r1, r3 = across(routed, 1), across(turned, 3)
    pieces, routed = lax.optimization_barrier((pieces, routed))
    total = jnp.sum(pieces, axis=0)
    pieces = lax.all_to_all(
        jnp.broadcast_to(total, pieces.shape), "space", 0, 0, tiled=True, axis_index_groups=groups
    )
    spread = pieces.reshape(width, cut)
    on1, on3 = r1[:cells // 2], r3[:cells // 2]
    spread, r1, r3, on1, on3 = lax.optimization_barrier((spread, r1, r3, on1, on3))
    swap = other_core(spread)
    g3 = across(spread[:, :width], 3)
    g1 = across(spread[:, :half], 1)
    g2 = across(spread[:, :half], 2)
    c0 = jnp.where(
        core == 0,
        jnp.concatenate([spread[:, width:], swap[:, width:]], axis=1),
        jnp.concatenate([swap[:, width:], spread[:, width:]], axis=1),
    )
    g1, g2, g3, c0, swap = lax.optimization_barrier((g1, g2, g3, c0, swap))
    mine = jnp.concatenate([g1, g2, g3], axis=1)
    crosses = [c0, across(c0, 1), across(c0, 2), across(c0, 3)]
    place = jnp.stack([run, core]).astype(jnp.int32)
    near, far, outer = level0(place, [spread, swap, mine, other_core(mine)], width)
    near, on1, on3 = lax.optimization_barrier((near, on1, on3))
    r2a, r2b = across(on1, 3), across(on3, 1)
    last = level1(place, near, far, outer, crosses, width, width // runs)
    return rotate(routed, r1, r2a, r2b, r3, near, far, last).T


def solution(mesh):
    in_specs = (P("space", "run"), P("run"), P())
    out_specs = P("space", "run")
    return jax.shard_map(body, mesh=mesh, in_specs=in_specs, out_specs=out_specs, check_vma=False)
```

```python
import functools
import math

import jax
import jax.numpy as jnp
from jax import lax
from jax.experimental import pallas as pl
from jax.experimental.pallas import tpu as pltpu
from jax.sharding import PartitionSpec as P

ITERS = 2
NS_STEPS = 8
BF = jnp.bfloat16
F32 = jnp.float32


def dot(a, b):
    return lax.dot_general(a, b, (((1,), (0,)), ((), ())), preferred_element_type=F32)


def dot_t(a, b):
    return lax.dot_general(a, b, (((0,), (0,)), ((), ())), preferred_element_type=F32)


def dot_nt(a, b):
    return lax.dot_general(a, b, (((1,), (1,)), ((), ())), preferred_element_type=F32)


def split(x):
    hi = x.astype(BF)
    return hi, (x - hi.astype(F32)).astype(BF)


def mul(a, b, op=dot):
    return op(a[0], b[0]) + (op(a[0], b[1]) + op(a[1], b[0]))


def half_mul(a, b, op=dot):
    return op(a[0], b) + op(a[1], b)


def half_mul_t(b, a):
    return dot_t(b, a[0]) + dot_t(b, a[1])


def solve(grams, eye):
    root = 1.0 / math.sqrt(2.0)
    gs = [(split(a), split(b), split(c)) for a, b, c in grams]
    heads = [((a + b) * root, (b.T + c) * root) for a, b, c in grams]
    for sweep in range(ITERS):
        scaled = []
        for pt, pb in heads:
            norm = lax.rsqrt(jnp.sum(pt * pt + pb * pb, keepdims=True) + 1e-06)
            scaled.append((split(pt * norm), split(pb * norm)))
        moments = [mul(st, st, dot_t) + mul(sb, sb, dot_t) for st, sb in scaled]
        turns = None
        ahead, fill = [], []
        for (a, b, c), (st, sb) in zip(gs, scaled):
            cell = [None] * 4
            ahead.append(cell)
            for n, f in enumerate((lambda a=a, st=st: mul(a, st), lambda b=b, sb=sb: mul(b, sb),
                                   lambda b=b, st=st: mul(b, st, dot_t), lambda c=c, sb=sb: mul(c, sb))):
                fill.append((cell, n, f))
        if sweep + 1 == ITERS:
            fill = []
        for k in range(NS_STEPS):
            last = k == NS_STEPS - 1
            halves = [split(m) for m in moments]
            weights = [1.5 * eye - 0.5 * m for m in moments]
            if not last:
                squares = [mul(h, h) for h in halves]
            turns = weights if k == 0 else [mul(split(t), split(w)) for t, w in zip(turns, weights)]
            for cell, n, f in fill[:len(grams)]:
                cell[n] = f()
            fill = fill[len(grams):]
            if not last:
                moments = [mul(h, split(2.25 * eye - 1.5 * m + 0.25 * q)) for h, m, q in zip(halves, moments, squares)]
        turns = [split(t) for t in turns]
        if sweep + 1 < ITERS:
            scaled = [(split(c[0] + c[1]), split(c[2] + c[3])) for c in ahead]
        heads = [(mul(st, t), mul(sb, t)) for (st, sb), t in zip(scaled, turns)]
    return heads


def identity(width):
    rows = lax.broadcasted_iota(jnp.int32, (width, width), 0)
    return (rows == lax.broadcasted_iota(jnp.int32, (width, width), 1)).astype(F32)


def level0_kernel(place_ref, *refs):
    parts, (near_ref, far_ref, outer_ref, own_ref, rest_ref, sems) = refs[:4], refs[4:]
    core = place_ref[1]
    copies = []
    for j, ref in enumerate((own_ref, rest_ref)):
        for k, slot in enumerate((core, 1 - core)):
            copies.append(pltpu.make_async_copy(parts[2 * j + k], ref.at[slot], sems.at[2 * j + k]))
    for c in copies:
        c.start()
    for c in copies:
        c.wait()
    width = near_ref.shape[1]
    half = width // 2

    def block(ref, n):
        at = slice(n * half, (n + 1) * half)
        return jnp.concatenate([ref[0, :, at], ref[1, :, at]], axis=1)

    near = (block(own_ref, 0), block(own_ref, 1), block(rest_ref, 0))
    far = (block(rest_ref, 2), block(rest_ref, 3), block(rest_ref, 1))
    grams = [near, far]
    bases = [(t.astype(BF), b.astype(BF)) for t, b in solve(grams, identity(width))]
    for i, ref in enumerate((near_ref, far_ref)):
        t, b = bases[i]
        ref[:width] = t
        ref[width:] = b
        g = [split(x) for x in grams[i]]
        up = half_mul(g[0], t) + half_mul(g[1], b)
        down = half_mul(g[1], t, dot_t) + half_mul(g[2], b)
        outer_ref[i] = half_mul_t(t, split(up)) + half_mul_t(b, split(down))


def level0(place, parts, width):
    half = width // 2
    return pl.pallas_call(
        level0_kernel,
        out_shape=[
            jax.ShapeDtypeStruct((2 * width, width), BF),
            jax.ShapeDtypeStruct((2 * width, width), BF),
            jax.ShapeDtypeStruct((2, width, width), F32),
        ],
        in_specs=[pl.BlockSpec(memory_space=pltpu.SMEM)] + [pl.BlockSpec(memory_space=pl.ANY)] * 4,
        scratch_shapes=[
            pltpu.VMEM((2, width, 3 * half), F32),
            pltpu.VMEM((2, width, 4 * half), F32),
            pltpu.SemaphoreType.DMA((4,)),
        ],
        compiler_params=pltpu.CompilerParams(vmem_limit_bytes=40 * 2**20),
        cost_estimate=pl.CostEstimate(flops=12 * 10**9, bytes_accessed=2 * 2**20, transcendentals=0),
        name="level0",
    )(place, *parts)


def level1_kernel(place_ref, near_ref, far_ref, outer_ref, c0_ref, c1_ref, c2_ref, c3_ref, last_ref, between_ref):
    run = place_ref[0]
    width = near_ref.shape[1]
    near = (near_ref[:width], near_ref[width:])
    far = (far_ref[width:], far_ref[:width])

    def between(first, second, f0, f1, s0, s1):
        (ft, fb), (st, sb) = first, second
        to_s1, to_s0, from_s0, from_s1 = (split(x[...]) for x in (f0, f1, s0, s1))
        up = half_mul(to_s1, sb) + half_mul(from_s1, st, dot_t)
        down = half_mul(to_s0, st) + half_mul(from_s0, sb, dot_t)
        return half_mul_t(ft, split(up)) + half_mul_t(fb, split(down))

    @pl.when(run < 2)
    def _():
        between_ref[...] = between(near, far, c0_ref, c1_ref, c2_ref, c3_ref)

    @pl.when(run >= 2)
    def _():
        between_ref[...] = between(far, near, c2_ref, c3_ref, c0_ref, c1_ref).T

    [(t, b)] = solve([(outer_ref[0], between_ref[...], outer_ref[1])], identity(width))
    quarter = last_ref.shape[0]
    pick_row = lax.broadcasted_iota(jnp.int32, (quarter, width), 0)
    pick_col = lax.broadcasted_iota(jnp.int32, (quarter, width), 1)
    pick = (pick_col == pick_row + run * quarter).astype(F32).astype(BF)
    last_ref[:, :width] = dot_nt(pick, t.astype(BF)).astype(BF)
    last_ref[:, width:] = dot_nt(pick, b.astype(BF)).astype(BF)


def level1(place, near, far, outer, crosses, width, quarter):
    return pl.pallas_call(
        level1_kernel,
        out_shape=jax.ShapeDtypeStruct((quarter, 2 * width), BF),
        in_specs=[pl.BlockSpec(memory_space=pltpu.SMEM)] + [pl.BlockSpec(memory_space=pltpu.VMEM)] * 7,
        out_specs=pl.BlockSpec(memory_space=pltpu.VMEM),
        scratch_shapes=[pltpu.VMEM((width, width), F32)],
        compiler_params=pltpu.CompilerParams(vmem_limit_bytes=40 * 2**20),
        cost_estimate=pl.CostEstimate(flops=8 * 10**9, bytes_accessed=2 * 2**20, transcendentals=0),
        name="level1",
    )(place, near, far, outer, *crosses)


def pack_kernel(shards, slots, counts_ref, rows_ref, out_ref, wide_ref):
    cells = rows_ref.shape[0]
    strips, _, lanes = wide_ref.shape
    pad = wide_ref.shape[1] - cells
    for h in range(strips):
        at = slice(h * lanes, (h + 1) * lanes)
        wide_ref[h, pl.ds(0, cells)] = rows_ref[:, at].astype(F32)
        wide_ref[h, pl.ds(cells, pad)] = jnp.zeros((pad, lanes), F32)

    def one(d, start):
        at = pl.ds(pl.multiple_of(d * slots, 16), slots)
        for h in range(strips):
            out_ref[at, h * lanes:(h + 1) * lanes] = wide_ref[h, pl.ds(start, slots)].astype(BF)
        return jnp.minimum(start + counts_ref[d], cells)

    lax.fori_loop(0, shards, one, jnp.int32(0), unroll=4)


def unpack_kernel(shards, slots, counts_ref, in_ref, out_ref, turned_ref, wide_ref):
    cells = out_ref.shape[0]
    half = cells // 2
    strips, _, lanes = wide_ref.shape

    def one(s, start):
        at = pl.ds(pl.multiple_of(s * slots, 16), slots)
        for h in range(strips):
            wide_ref[h, pl.ds(start, slots)] = in_ref[at, h * lanes:(h + 1) * lanes].astype(F32)
        return jnp.minimum(start + counts_ref[s], cells)

    lax.fori_loop(0, shards, one, jnp.int32(0), unroll=4)
    for h in range(strips):
        at = slice(h * lanes, (h + 1) * lanes)
        for k in range(2):
            rows = wide_ref[h, pl.ds(k * half, half)].astype(BF)
            out_ref[pl.ds(k * half, half), at] = rows
            turned_ref[pl.ds((1 - k) * half, half), at] = rows


def rotate_kernel(own, p1, p2a, p2b, p3, near_ref, far_ref, last_ref, out_ref):
    step, steps = pl.program_id(0), pl.num_programs(0)
    cells, width = own.shape
    tile = out_ref.shape[1]
    half = cells // 2
    first = pl.multiple_of(step * tile, tile)

    def turn(p2, inside, other):
        at = pl.ds(first, tile)
        near = (dot(own[at], near_ref[:width]) + dot(p1[at], near_ref[width:])).astype(BF)
        rows = p2[pl.ds(pl.multiple_of(inside, tile), tile)]
        mate = p3[pl.ds(pl.multiple_of(other, tile), tile)]
        far = (dot(mate, far_ref[:width]) + dot(rows, far_ref[width:])).astype(BF)
        out_ref[...] = (dot_nt(last_ref[:, :width], near) + dot_nt(last_ref[:, width:], far)).astype(BF)

    @pl.when(step < steps // 2)
    def _():
        turn(p2a, first, first + half)

    @pl.when(step >= steps // 2)
    def _():
        turn(p2b, first - half, first - half)


def rotate(own, p1, p2a, p2b, p3, near, far, last):
    quarter, steps = last.shape[0], 2
    cells = own.shape[0]
    return pl.pallas_call(
        rotate_kernel,
        grid=(steps,),
        out_shape=jax.ShapeDtypeStruct((quarter, cells), BF),
        in_specs=[pl.BlockSpec(memory_space=pltpu.VMEM)] * 8,
        out_specs=pl.BlockSpec((quarter, cells // steps), lambda i: (0, i)),
        compiler_params=pltpu.CompilerParams(vmem_limit_bytes=40 * 2**20),
        name="rotate",
    )(own, p1, p2a, p2b, p3, near, far, last)


def local_call(kernel, shapes, specs, scratch, name):
    outs = [jax.ShapeDtypeStruct(shape, BF) for shape in shapes]
    return pl.pallas_call(
        kernel,
        out_shape=outs,
        in_specs=[pl.BlockSpec(memory_space=m) for m in specs],
        out_specs=[pl.BlockSpec(memory_space=pltpu.VMEM) for _ in outs],
        scratch_shapes=scratch,
        compiler_params=pltpu.CompilerParams(vmem_limit_bytes=40 * 2**20),
        name=name,
    )


def body(snapshots, run_counts, route_counts):
    cells, width = snapshots.shape
    shards = lax.axis_size("space")
    runs = lax.axis_size("run")
    slots = 3 * cells // (2 * shards)
    run = lax.axis_index("run")
    spot = lax.axis_index("space")
    core = lax.rem(spot, 2)
    groups = [[2 * i + c for i in range(shards // 2)] for c in range(2)]

    def across(x, mask):
        return lax.ppermute(x, "run", [(r, r ^ mask) for r in range(runs)])

    def other_core(x):
        return lax.ppermute(x, "space", [(s, s ^ 1) for s in range(shards)])

    send = lax.dynamic_index_in_dim(route_counts, spot, 0, keepdims=False)
    recv = lax.dynamic_index_in_dim(route_counts, spot, 1, keepdims=False)
    smem, vmem = pltpu.SMEM, pltpu.VMEM
    wide = [pltpu.VMEM((width // 128, cells + 64, 128), F32)]
    keep = jnp.arange(width, dtype=jnp.int32) < run_counts[0]
    own = jnp.where(keep[None, :], snapshots, jnp.zeros((), BF))
    p1, p3 = across(own, 1), across(own, 3)
    [packed] = local_call(
        functools.partial(pack_kernel, shards, slots), [(shards * slots, width)], [smem, vmem], wide, "pack"
    )(send, own)
    arrived = lax.all_to_all(packed.reshape(shards, slots, width), "space", 0, 0, tiled=True)

    left = jnp.where(run < 2, own, p1)
    blocks = [dot_t(own, own), dot_t(own, p1), dot_t(left, p3)]
    half = width // 2

    def side(first):
        return jnp.concatenate([jnp.where(first, b[:, :half], b[:, half:]) for b in blocks], axis=1)

    mine = side(core == 0) + other_core(side(core == 1))
    mine, arrived = lax.optimization_barrier((mine, arrived))
    cut = mine.shape[1]
    routed, turned = local_call(
        functools.partial(unpack_kernel, shards, slots), [(cells, width)] * 2, [smem, vmem], wide, "unpack"
    )(recv, arrived.reshape(shards * slots, width))
    pieces = mine.reshape(shards // 2, -1, cut)
    pieces = lax.all_to_all(pieces, "space", 0, 0, tiled=True, axis_index_groups=groups)
    r1, r3 = across(routed, 1), across(turned, 3)
    pieces, routed = lax.optimization_barrier((pieces, routed))
    total = jnp.sum(pieces, axis=0)
    pieces = lax.all_to_all(
        jnp.broadcast_to(total, pieces.shape), "space", 0, 0, tiled=True, axis_index_groups=groups
    )
    spread = pieces.reshape(width, cut)
    on1, on3 = r1[:cells // 2], r3[:cells // 2]
    spread, r1, r3, on1, on3 = lax.optimization_barrier((spread, r1, r3, on1, on3))
    swap = other_core(spread)
    g3 = across(spread[:, :width], 3)
    g1 = across(spread[:, :half], 1)
    g2 = across(spread[:, :half], 2)
    c0 = jnp.where(
        core == 0,
        jnp.concatenate([spread[:, width:], swap[:, width:]], axis=1),
        jnp.concatenate([swap[:, width:], spread[:, width:]], axis=1),
    )
    g1, g2, g3, c0, swap = lax.optimization_barrier((g1, g2, g3, c0, swap))
    mine = jnp.concatenate([g1, g2, g3], axis=1)
    crosses = [c0, across(c0, 1), across(c0, 2), across(c0, 3)]
    place = jnp.stack([run, core]).astype(jnp.int32)
    near, far, outer = level0(place, [spread, swap, mine, other_core(mine)], width)
    near, on1, on3 = lax.optimization_barrier((near, on1, on3))
    r2a, r2b = across(on1, 3), across(on3, 1)
    last = level1(place, near, far, outer, crosses, width, width // runs)
    return rotate(routed, r1, r2a, r2b, r3, near, far, last).T


def solution(mesh):
    in_specs = (P("space", "run"), P("run"), P())
    out_specs = P("space", "run")
    return jax.shard_map(body, mesh=mesh, in_specs=in_specs, out_specs=out_specs, check_vma=False)
```
